512 devices in a mesh: row: 16 (over y, core), col: 32 (over z, x).
Axes of the slice: x: 4, y: 8, z: 8, core: 2. Of those that a mesh axis runs over, the one named last changes fastest.
Arguments:
- inverse_top: bfloat16 [12288, 12288], P('row', 'col'), may hold values from -0.0546875 to 0.0546875
- inverse_mid: bfloat16 [2, 8192, 8192], P(None, 'row', 'col'), may hold values from -0.0625 to 0.0625
- inverse_low: bfloat16 [4, 8192, 8192], P(None, 'row', 'col'), may hold values from -0.0625 to 0.0625
- coupling_mid: bfloat16 [2, 4096, 8192], P(None, 'col', 'row'), may hold values from -0.0625 to 0.0625
- coupling_low: bfloat16 [4, 4096, 8192], P(None, 'col', 'row'), may hold values from -0.0625 to 0.0625
- source_top: float32 [12288, 16], P('col'), may hold values from -6 to 6
- source_mid: float32 [2, 8192, 16], P(None, 'col'), may hold values from -6 to 6
- source_low: float32 [4, 8192, 16], P(None, 'col'), may hold values from -6 to 6
- pivots_top: float32 [12288], P('row'), may hold values from -1.5 to 1.5
- pivots_mid: float32 [2, 8192], P(None, 'row'), may hold values from -1.5 to 1.5
- pivots_low: float32 [4, 8192], P(None, 'row'), may hold values from -1.5 to 1.5
- sizes_mid: int32 [2], replicated, may hold values from 4096 to 8192, as said below
- sizes_low: int32 [4], replicated, may hold values from 4096 to 8192, as said below
- blocks_mid: int32 [2, 32], replicated, may hold values from 0 to 95, as said below
- blocks_low: int32 [4, 32], replicated, may hold values from 0 to 63, as said below
Outputs:
- solution_top: float32 [12288, 16], P('col')
- solution_mid: float32 [2, 8192, 16], P(None, 'col')
- solution_low: float32 [4, 8192, 16], P(None, 'col')
The draws below stay inside these ranges and needn't reach their ends.
Inputs may be any that keep to these rules, and one draw needn't show every extreme that they name: `sizes_mid`: one front of the level has used order exactly 8192, the other at least half of it. `sizes_low`: one front of the level has used order exactly 8192, the others at least half of it. `blocks_mid`: each list names distinct blocks in no particular order, the parent's last block among them. `blocks_low`: each list names distinct blocks in no particular order, the parent's last block among them.
All inputs are finite; a program needn't handle non-finite values.
Results may differ from the reference program's by a relative error of at most 0.015.
Values may be sent and summed in bfloat16 or wider, within the bound.
No kernel may reach another device: no remote copies, remote signals or barrier semaphores. Data moves between devices by JAX's collectives and lax.ppermute only.
A program may use at most 64 MiB of HBM per device.

```python
import jax
import jax.numpy as jnp

S0 = 12288
S1 = 8192
S2 = 8192
U1 = 4096
U2 = 4096
BLOCK = 128
NRHS = 16


def front_sizes(key, count, full):
    values = jax.random.randint(key, (count,), full // 2, full + 1)
    chosen = jax.random.randint(jax.random.fold_in(key, 7), (), 0, count)
    return jnp.where(jnp.arange(count) == chosen, full, values).astype(jnp.int32)


def block_lists(key, count, picks, total):
    keys = jax.random.split(key, count)

    def single(entry):
        order = jax.random.permutation(entry, total - 1).astype(jnp.int32)
        tail = jnp.full((1,), total - 1, jnp.int32)
        listed = jnp.concatenate([order[:picks - 1], tail])
        return jax.random.permutation(jax.random.fold_in(entry, 11), listed)
    return jax.vmap(single)(keys).astype(jnp.int32)


def draw_sizes_mid(key, part):
    key = jax.random.fold_in(key, 1)
    return front_sizes(key, 2, S1)


def draw_sizes_low(key, part):
    key = jax.random.fold_in(key, 2)
    return front_sizes(key, 4, S2)


def draw_blocks_mid(key, part):
    key = jax.random.fold_in(key, 3)
    return block_lists(key, 2, U1 // BLOCK, S0 // BLOCK)


def draw_blocks_low(key, part):
    key = jax.random.fold_in(key, 4)
    return block_lists(key, 4, U2 // BLOCK, S1 // BLOCK)


def levels(key, shape, cuts, low, largest):
    def one(dim, blocks):
        draws = jax.random.uniform(jax.random.fold_in(jax.random.fold_in(key, 6), dim), (blocks,), jnp.float32, low / len(cuts), largest / len(cuts))
        return jnp.repeat(jnp.exp(draws), shape[dim] // blocks).reshape((-1,) + (1,) * (len(shape) - dim - 1))

    level = one(*cuts[0])
    for cut in cuts[1:]:
        level = level * one(*cut)
    return level


def noise(stream_key, dims, scale, reach, cuts=(), kind=jnp.bfloat16):
    values = scale * jax.random.normal(stream_key, dims, jnp.float32)
    if cuts:
        values = values * levels(stream_key, dims, cuts, -0.22, 0.18)
    return jnp.clip(values, -reach, reach).astype(kind)


def setup_inputs(seed: int = 0) -> dict:
    splits = jax.random.split(jax.random.key(seed), 16)
    return {
        "inverse_top": noise(splits[0], (S0, S0), S0 ** -0.5, 0.0546875, ((0, 16), (1, 32))),
        "inverse_mid": noise(splits[1], (2, S1, S1), S1 ** -0.5, 0.0625, ((1, 16), (2, 32))),
        "inverse_low": noise(splits[2], (4, S2, S2), S2 ** -0.5, 0.0625, ((1, 16), (2, 32))),
        "coupling_mid": noise(splits[3], (2, U1, S1), S1 ** -0.5, 0.0625, ((1, 32), (2, 16))),
        "coupling_low": noise(splits[4], (4, U2, S2), S2 ** -0.5, 0.0625, ((1, 32), (2, 16))),
        "source_top": noise(splits[5], (S0, NRHS), 1.0, 6.0, ((0, 32),), jnp.float32),
        "source_mid": noise(splits[6], (2, S1, NRHS), 1.0, 6.0, ((1, 32),), jnp.float32),
        "source_low": noise(splits[7], (4, S2, NRHS), 1.0, 6.0, ((1, 32),), jnp.float32),
        "pivots_top": jnp.clip(jax.random.uniform(splits[8], (S0,), jnp.float32, -1.5, 1.5) * levels(splits[8], (S0,), ((0, 16),), -0.4, 0.0), -1.5, 1.5),
        "pivots_mid": jnp.clip(jax.random.uniform(splits[9], (2, S1), jnp.float32, -1.5, 1.5) * levels(splits[9], (2, S1), ((1, 16),), -0.4, 0.0), -1.5, 1.5),
        "pivots_low": jnp.clip(jax.random.uniform(splits[10], (4, S2), jnp.float32, -1.5, 1.5) * levels(splits[10], (4, S2), ((1, 16),), -0.4, 0.0), -1.5, 1.5),
        "sizes_mid": draw_sizes_mid(jax.random.fold_in(splits[15], 71), 0),
        "sizes_low": draw_sizes_low(jax.random.fold_in(splits[15], 71), 0),
        "blocks_mid": draw_blocks_mid(jax.random.fold_in(splits[15], 71), 0),
        "blocks_low": draw_blocks_low(jax.random.fold_in(splits[15], 71), 0),
    }


def masks(sizes, total):
    index = jnp.arange(total, dtype=jnp.int32)
    return (index[None, :] < sizes[:, None]).astype(jnp.float32)[:, :, None]


def front_dot(matrices, vectors, transpose):
    result = []
    for front in range(matrices.shape[0]):
        matrix = matrices[front].T if transpose else matrices[front]
        result.append(jnp.dot(matrix, vectors[front], preferred_element_type=jnp.float32))
    return jnp.stack(result)


def place(update, blocks, parent_rows):
    fronts, urows, width = update.shape
    tiles = update.reshape(fronts, urows // BLOCK, BLOCK, width).astype(jnp.float32)
    placed = jnp.zeros((fronts, parent_rows // BLOCK, BLOCK, width), jnp.float32)
    front_ids = jnp.arange(fronts, dtype=jnp.int32)[:, None]
    placed = placed.at[front_ids, blocks].add(tiles)
    placed = placed.reshape(fronts // 2, 2, parent_rows, width)
    return placed[:, 0] + placed[:, 1]


def pick(solved, blocks):
    parents, prows, width = solved.shape
    tiles = solved.reshape(parents, prows // BLOCK, BLOCK, width)
    parent_ids = (jnp.arange(blocks.shape[0], dtype=jnp.int32) // 2)[:, None]
    chosen = tiles[parent_ids, blocks]
    return chosen.reshape(blocks.shape[0], blocks.shape[1] * BLOCK, width)


def reference(inverse_top, inverse_mid, inverse_low, coupling_mid, coupling_low, source_top, source_mid, source_low, pivots_top, pivots_mid, pivots_low, sizes_mid, sizes_low, blocks_mid, blocks_low):
    inverses = [inverse_top[None], inverse_mid, inverse_low]
    couplings = [None, coupling_mid, coupling_low]
    sources = [source_top[None], source_mid, source_low]
    pivots = [pivots_top[None], pivots_mid, pivots_low]
    sizes = [jnp.full((1,), S0, jnp.int32), sizes_mid, sizes_low]
    lists = [None, blocks_mid, blocks_low]
    marks = [masks(sizes[level], inverses[level].shape[1]) for level in range(3)]
    scaled = [None, None, None]
    residual = sources[2]
    for level in (2, 1, 0):
        solved = marks[level] * front_dot(inverses[level], (marks[level] * residual).astype(jnp.bfloat16), False)
        scaled[level] = solved * pivots[level][:, :, None]
        if level > 0:
            update = front_dot(couplings[level], solved.astype(jnp.bfloat16), False)
            residual = sources[level - 1] - place(update, lists[level], sources[level - 1].shape[1])
    outputs = [None, None, None]
    carried = None
    for level in range(3):
        residual = scaled[level] if level == 0 else scaled[level] - carried
        solved = marks[level] * front_dot(inverses[level], (marks[level] * residual).astype(jnp.bfloat16), True)
        outputs[level] = solved
        if level < 2:
            picked = pick(solved.astype(jnp.bfloat16), lists[level + 1])
            carried = front_dot(couplings[level + 1], picked, True)
    return outputs[0][0], outputs[1], outputs[2]
```

```python
import jax
import jax.numpy as jnp
from jax import lax
from jax.sharding import PartitionSpec as P

BLOCK = 128
BF16 = jnp.bfloat16
F32 = jnp.float32


def level_mask(sizes, count, start):
    index = start + jnp.arange(count, dtype=jnp.int32)
    return (index[None, :] < sizes[:, None]).astype(F32)[:, None, :]


def exchange(value, axis, masks):
    size = lax.axis_size(axis)
    return [lax.ppermute(value, axis, [(i, i ^ m) for i in range(size)]) for m in masks]


def sum_stage(partial, axis, masks):
    own = partial.astype(BF16)
    parts = [own] + exchange(own, axis, masks)
    parts = [part.astype(F32) for part in parts]
    while len(parts) > 1:
        parts = [parts[i] + parts[i + 1] for i in range(0, len(parts), 2)]
    return parts[0]


def sum_over_col(partial):
    size = lax.axis_size("col")
    step = 1
    while step < size:
        if step * 4 <= size:
            masks = (step, 2 * step, 3 * step)
            partial = sum_stage(partial, "col", masks)
            step *= 4
        else:
            partial = sum_stage(partial, "col", (step,))
            step *= 2
    return partial


def spread(value, axis):
    size = lax.axis_size(axis)
    copies = jnp.broadcast_to(value.astype(BF16)[None], (size,) + value.shape)
    return lax.all_to_all(copies, axis, 0, 0, tiled=True)


def sum_over_row(partial):
    return jnp.sum(spread(partial, "row").astype(F32), axis=0)


def times_rows(matrix, vector):
    return jnp.einsum("fij,fcj->fci", matrix, vector.astype(BF16), preferred_element_type=F32)


def times_columns(matrix, vector):
    return jnp.einsum("fij,fci->fcj", matrix, vector.astype(BF16), preferred_element_type=F32)


def place_updates(update, blocks, parent_local):
    whole = spread(update, "col")
    count, fronts, width, _ = whole.shape
    local_blocks = parent_local // BLOCK
    targets = lax.axis_index("col") * local_blocks + jnp.arange(local_blocks, dtype=jnp.int32)
    select = (blocks.T[:, :, None] == targets[None, None, :]).astype(F32)
    placed = []
    for b in range(local_blocks):
        terms = select[:, :, b][:, :, None, None] * whole.astype(F32)
        summed = jnp.sum(terms.reshape(count, fronts // 2, 2, width, BLOCK), axis=(0, 2))
        placed.append(summed)
    return jnp.concatenate(placed, axis=-1)


def child_rows(solved, blocks):
    whole = spread(solved, "col")
    _, parents, width, plocal = whole.shape
    local_blocks = plocal // BLOCK
    children = blocks.shape[0]
    mine = lax.dynamic_slice_in_dim(blocks, lax.axis_index("col"), 1, 1)[:, 0]
    picked = []
    for c in range(children):
        at = (mine[c] // local_blocks, c // 2, 0, (mine[c] % local_blocks) * BLOCK)
        picked.append(lax.dynamic_slice(whole, at, (1, 1, width, BLOCK))[0])
    return jnp.concatenate(picked, axis=0)


def sweep(inverses, couplings, sources, pivots, sizes, lists):
    depth = len(inverses)
    row_at = lax.axis_index("row")
    col_at = lax.axis_index("col")
    row_masks = []
    col_masks = []
    for level in range(depth):
        fronts, rows_here, cols_here = inverses[level].shape
        row_masks.append(level_mask(sizes[level], rows_here, row_at * rows_here))
        col_masks.append(level_mask(sizes[level], cols_here, col_at * cols_here))
    scaled = [None] * depth
    residual = sources[depth - 1]
    for level in range(depth - 1, -1, -1):
        solved = sum_over_col(times_rows(inverses[level], residual * col_masks[level]))
        solved = solved * row_masks[level]
        scaled[level] = solved * pivots[level][:, None, :]
        if level > 0:
            update = sum_over_row(times_rows(couplings[level], solved))
            residual = sources[level - 1] - place_updates(
                update, lists[level], sources[level - 1].shape[-1]
            )
    outputs = [None] * depth
    carried = None
    for level in range(depth):
        residual = scaled[level] if level == 0 else scaled[level] - carried
        solved = sum_over_row(times_columns(inverses[level], residual * row_masks[level]))
        solved = solved * col_masks[level]
        outputs[level] = solved
        if level + 1 < depth:
            picked = child_rows(solved, lists[level + 1])
            carried = sum_over_col(times_columns(couplings[level + 1], picked))
    return outputs


def local(
    inverse_top,
    inverse_mid,
    inverse_low,
    coupling_mid,
    coupling_low,
    source_top,
    source_mid,
    source_low,
    pivots_top,
    pivots_mid,
    pivots_low,
    sizes_mid,
    sizes_low,
    blocks_mid,
    blocks_low,
):
    inverses = [inverse_top[None], inverse_mid, inverse_low]
    couplings = [None, coupling_mid, coupling_low]
    pivots = [pivots_top[None], pivots_mid, pivots_low]
    root_order = inverse_top.shape[0] * lax.axis_size("row")
    sizes = [jnp.full((1,), root_order, jnp.int32), sizes_mid, sizes_low]
    lists = [None, blocks_mid, blocks_low]
    sources = [source_top[None], source_mid, source_low]
    sources = [jnp.swapaxes(source, 1, 2) for source in sources]
    outputs = sweep(inverses, couplings, sources, pivots, sizes, lists)
    outputs = [jnp.swapaxes(output, 1, 2) for output in outputs]
    return (outputs[0][0], outputs[1], outputs[2])


def solution(mesh):
    placed = (
        P("row", "col"),
        P(None, "row", "col"),
        P(None, "row", "col"),
        P(None, "col", "row"),
        P(None, "col", "row"),
        P("col", None),
        P(None, "col", None),
        P(None, "col", None),
        P("row"),
        P(None, "row"),
        P(None, "row"),
        P(),
        P(),
        P(),
        P(),
    )
    return jax.shard_map(
        local,
        mesh=mesh,
        in_specs=placed,
        out_specs=(P("col", None), P(None, "col", None), P(None, "col", None)),
        check_vma=False,
    )
```

```python
import jax
import jax.numpy as jnp
from jax import lax
from jax.sharding import PartitionSpec as P

BLOCK = 128
BF16 = jnp.bfloat16
F32 = jnp.float32


def level_mask(sizes, count, start):
    index = start + jnp.arange(count, dtype=jnp.int32)
    return (index[None, :] < sizes[:, None]).astype(F32)[:, None, :]


def exchange(value, axis, masks):
    size = lax.axis_size(axis)
    return [lax.ppermute(value, axis, [(i, i ^ m) for i in range(size)]) for m in masks]


def sum_stage(partial, axis, masks):
    own = partial.astype(BF16)
    parts = [own] + exchange(own, axis, masks)
    parts = [part.astype(F32) for part in parts]
    while len(parts) > 1:
        parts = [parts[i] + parts[i + 1] for i in range(0, len(parts), 2)]
    return parts[0]


def near_groups():
    size = lax.axis_size("col")
    return [[z * 4 + x for x in range(4)] for z in range(size // 4)]


def far_groups():
    size = lax.axis_size("col")
    return [[z * 4 + x for z in range(size // 4)] for x in range(4)]


def sum_groups(partial, groups):
    size = len(groups[0])
    copies = jnp.broadcast_to(partial.astype(BF16)[None], (size,) + partial.shape)
    parts = lax.all_to_all(copies, "col", 0, 0, axis_index_groups=groups, tiled=True)
    return jnp.sum(parts.astype(F32), axis=0)


def sum_near_far(partial):
    return sum_groups(sum_groups(partial, near_groups()), far_groups())


def sum_permutes_far(partial):
    return sum_groups(sum_stage(partial, "col", (1, 2, 3)), far_groups())


def sum_scattered(partial):
    size = lax.axis_size("col")
    fronts, width, count = partial.shape
    pieces = partial.astype(BF16).reshape(size, 1, fronts * width * count // size)
    pieces = lax.all_to_all(pieces, "col", 0, 0, tiled=True)
    mine = jnp.sum(pieces.astype(F32), axis=0)
    return spread(mine, "col").astype(F32).reshape(fronts, width, count)


def spread(value, axis):
    size = lax.axis_size(axis)
    copies = jnp.broadcast_to(value.astype(BF16)[None], (size,) + value.shape)
    return lax.all_to_all(copies, axis, 0, 0, tiled=True)


def sum_over_row(partial):
    return jnp.sum(spread(partial, "row").astype(F32), axis=0)


def times_rows(matrix, vector):
    return jnp.einsum("fij,fcj->fci", matrix, vector.astype(BF16), preferred_element_type=F32)


def times_columns(matrix, vector):
    return jnp.einsum("fij,fci->fcj", matrix, vector.astype(BF16), preferred_element_type=F32)


def place_updates(update, blocks, parent_local):
    whole = spread(update, "col")
    count, fronts, width, _ = whole.shape
    local_blocks = parent_local // BLOCK
    targets = lax.axis_index("col") * local_blocks + jnp.arange(local_blocks, dtype=jnp.int32)
    select = (blocks.T[:, :, None] == targets[None, None, :]).astype(F32)
    placed = []
    for b in range(local_blocks):
        terms = select[:, :, b][:, :, None, None] * whole.astype(F32)
        summed = jnp.sum(terms.reshape(count, fronts // 2, 2, width, BLOCK), axis=(0, 2))
        placed.append(summed)
    return jnp.concatenate(placed, axis=-1)


def child_rows(solved, blocks):
    whole = spread(solved, "col")
    _, parents, width, plocal = whole.shape
    local_blocks = plocal // BLOCK
    children = blocks.shape[0]
    mine = lax.dynamic_slice_in_dim(blocks, lax.axis_index("col"), 1, 1)[:, 0]
    picked = []
    for c in range(children):
        at = (mine[c] // local_blocks, c // 2, 0, (mine[c] % local_blocks) * BLOCK)
        picked.append(lax.dynamic_slice(whole, at, (1, 1, width, BLOCK))[0])
    return jnp.concatenate(picked, axis=0)


def sweep(inverses, couplings, sources, pivots, sizes, lists):
    depth = len(inverses)
    row_at = lax.axis_index("row")
    col_at = lax.axis_index("col")
    row_masks = []
    col_masks = []
    for level in range(depth):
        fronts, rows_here, cols_here = inverses[level].shape
        row_masks.append(level_mask(sizes[level], rows_here, row_at * rows_here))
        col_masks.append(level_mask(sizes[level], cols_here, col_at * cols_here))
    scaled = [None] * depth
    residual = sources[depth - 1]
    forward = [sum_scattered, sum_near_far, sum_near_far]
    backward = [sum_permutes_far, sum_scattered]
    for level in range(depth - 1, -1, -1):
        solved = forward[level](times_rows(inverses[level], residual * col_masks[level]))
        solved = solved * row_masks[level]
        scaled[level] = solved * pivots[level][:, None, :]
        if level > 0:
            update = sum_over_row(times_rows(couplings[level], solved))
            residual = sources[level - 1] - place_updates(
                update, lists[level], sources[level - 1].shape[-1]
            )
    outputs = [None] * depth
    carried = None
    for level in range(depth):
        residual = scaled[level] if level == 0 else scaled[level] - carried
        solved = sum_over_row(times_columns(inverses[level], residual * row_masks[level]))
        solved = solved * col_masks[level]
        outputs[level] = solved
        if level + 1 < depth:
            picked = child_rows(solved, lists[level + 1])
            carried = backward[level](times_columns(couplings[level + 1], picked))
    return outputs


def local(
    inverse_top,
    inverse_mid,
    inverse_low,
    coupling_mid,
    coupling_low,
    source_top,
    source_mid,
    source_low,
    pivots_top,
    pivots_mid,
    pivots_low,
    sizes_mid,
    sizes_low,
    blocks_mid,
    blocks_low,
):
    inverses = [inverse_top[None], inverse_mid, inverse_low]
    couplings = [None, coupling_mid, coupling_low]
    pivots = [pivots_top[None], pivots_mid, pivots_low]
    root_order = inverse_top.shape[0] * lax.axis_size("row")
    sizes = [jnp.full((1,), root_order, jnp.int32), sizes_mid, sizes_low]
    lists = [None, blocks_mid, blocks_low]
    sources = [source_top[None], source_mid, source_low]
    sources = [jnp.swapaxes(source, 1, 2) for source in sources]
    outputs = sweep(inverses, couplings, sources, pivots, sizes, lists)
    outputs = [jnp.swapaxes(output, 1, 2) for output in outputs]
    return (outputs[0][0], outputs[1], outputs[2])


def solution(mesh):
    placed = (
        P("row", "col"),
        P(None, "row", "col"),
        P(None, "row", "col"),
        P(None, "col", "row"),
        P(None, "col", "row"),
        P("col", None),
        P(None, "col", None),
        P(None, "col", None),
        P("row"),
        P(None, "row"),
        P(None, "row"),
        P(),
        P(),
        P(),
        P(),
    )
    return jax.shard_map(
        local,
        mesh=mesh,
        in_specs=placed,
        out_specs=(P("col", None), P(None, "col", None), P(None, "col", None)),
        check_vma=False,
    )
```

```python
import jax
import jax.numpy as jnp
from jax import lax
from jax.sharding import PartitionSpec as P

BLOCK = 128
BF16 = jnp.bfloat16
F32 = jnp.float32


def level_mask(sizes, count, start):
    index = start + jnp.arange(count, dtype=jnp.int32)
    return (index[None, :] < sizes[:, None]).astype(F32)[:, None, :]


def near_groups():
    size = lax.axis_size("col")
    return [[z * 4 + x for x in range(4)] for z in range(size // 4)]


def far_groups():
    size = lax.axis_size("col")
    return [[z * 4 + x for z in range(size // 4)] for x in range(4)]


def sum_groups(partial, groups):
    size = len(groups[0])
    copies = jnp.broadcast_to(partial.astype(BF16)[None], (size,) + partial.shape)
    parts = lax.all_to_all(copies, "col", 0, 0, axis_index_groups=groups, tiled=True)
    return jnp.sum(parts.astype(F32), axis=0)


def sum_near_far(partial):
    return sum_groups(sum_groups(partial, near_groups()), far_groups())


def sum_scattered(partial):
    size = lax.axis_size("col")
    fronts, width, count = partial.shape
    pieces = partial.astype(BF16).reshape(size, 1, fronts * width * count // size)
    pieces = lax.all_to_all(pieces, "col", 0, 0, tiled=True)
    mine = jnp.sum(pieces.astype(F32), axis=0)
    return spread(mine, "col").astype(F32).reshape(fronts, width, count)


def spread(value, axis):
    size = lax.axis_size(axis)
    copies = jnp.broadcast_to(value.astype(BF16)[None], (size,) + value.shape)
    return lax.all_to_all(copies, axis, 0, 0, tiled=True)


def sum_over_row(partial):
    return jnp.sum(spread(partial, "row").astype(F32), axis=0)


def times_rows(matrix, vector):
    return jnp.einsum("fij,fcj->fci", matrix, vector.astype(BF16), preferred_element_type=F32)


def times_columns(matrix, vector):
    return jnp.einsum("fij,fci->fcj", matrix, vector.astype(BF16), preferred_element_type=F32)


def place_updates(update, blocks, parent_local):
    whole = spread(update, "col")
    count, fronts, width, _ = whole.shape
    local_blocks = parent_local // BLOCK
    targets = lax.axis_index("col") * local_blocks + jnp.arange(local_blocks, dtype=jnp.int32)
    select = (blocks.T[:, :, None] == targets[None, None, :]).astype(F32)
    placed = []
    for b in range(local_blocks):
        terms = select[:, :, b][:, :, None, None] * whole.astype(F32)
        summed = jnp.sum(terms.reshape(count, fronts // 2, 2, width, BLOCK), axis=(0, 2))
        placed.append(summed)
    return jnp.concatenate(placed, axis=-1)


def own_rows(coupling, blocks, parent_local):
    whole = lax.all_gather(coupling, "col", axis=0)
    local_blocks = parent_local // BLOCK
    targets = lax.axis_index("col") * local_blocks + jnp.arange(local_blocks, dtype=jnp.int32)
    hits = (blocks[:, None, :] == targets[None, :, None]).astype(jnp.int32)
    listed = jnp.sum(hits, axis=-1)
    at = jnp.sum(hits * jnp.arange(blocks.shape[1], dtype=jnp.int32), axis=-1)
    rows = []
    for c in range(blocks.shape[0]):
        for b in range(local_blocks):
            start = (at[c, b], c, 0, 0)
            rows.append(lax.dynamic_slice(whole, start, (1, 1) + coupling.shape[1:])[0, 0])
    rows = jnp.stack(rows).reshape((blocks.shape[0], parent_local) + coupling.shape[2:])
    return rows, jnp.repeat(listed.astype(F32), BLOCK, axis=1)[:, None, :]


def own_update(rows, listed, solved):
    partial = times_rows(rows, solved) * listed
    children, width, count = partial.shape
    return sum_over_row(jnp.sum(partial.reshape(children // 2, 2, width, count), axis=1))


def own_carried(rows, listed, solved, total):
    taken = jnp.repeat(solved, 2, axis=0) * listed
    return total(times_columns(rows, taken))


def sweep(inverses, couplings, sources, pivots, sizes, lists):
    depth = len(inverses)
    row_at = lax.axis_index("row")
    col_at = lax.axis_index("col")
    row_masks = []
    col_masks = []
    moved = [None] * depth
    for level in range(depth):
        fronts, rows_here, cols_here = inverses[level].shape
        row_masks.append(level_mask(sizes[level], rows_here, row_at * rows_here))
        col_masks.append(level_mask(sizes[level], cols_here, col_at * cols_here))
        if level > 0:
            coupling = couplings[level]
            if level > 1:
                coupling, _ = lax.optimization_barrier((coupling, moved[level - 1]))
            moved[level] = own_rows(coupling, lists[level], inverses[level - 1].shape[2])
    scaled = [None] * depth
    residual = sources[depth - 1]
    forward = [sum_near_far, sum_near_far, sum_scattered]
    backward = [sum_near_far, sum_scattered]
    for level in range(depth - 1, -1, -1):
        solved = forward[level](times_rows(inverses[level], residual * col_masks[level]))
        solved = solved * row_masks[level]
        scaled[level] = solved * pivots[level][:, None, :]
        if level > 1:
            update = sum_over_row(times_rows(couplings[level], solved))
            residual = sources[level - 1] - place_updates(
                update, lists[level], sources[level - 1].shape[-1]
            )
        elif level > 0:
            residual = sources[level - 1] - own_update(*moved[level], solved)
    outputs = [None] * depth
    carried = None
    for level in range(depth):
        residual = scaled[level] if level == 0 else scaled[level] - carried
        solved = sum_over_row(times_columns(inverses[level], residual * row_masks[level]))
        solved = solved * col_masks[level]
        outputs[level] = solved
        if level + 1 < depth:
            carried = own_carried(*moved[level + 1], solved, backward[level])
    return outputs


def local(
    inverse_top,
    inverse_mid,
    inverse_low,
    coupling_mid,
    coupling_low,
    source_top,
    source_mid,
    source_low,
    pivots_top,
    pivots_mid,
    pivots_low,
    sizes_mid,
    sizes_low,
    blocks_mid,
    blocks_low,
):
    inverses = [inverse_top[None], inverse_mid, inverse_low]
    couplings = [None, coupling_mid, coupling_low]
    pivots = [pivots_top[None], pivots_mid, pivots_low]
    root_order = inverse_top.shape[0] * lax.axis_size("row")
    sizes = [jnp.full((1,), root_order, jnp.int32), sizes_mid, sizes_low]
    lists = [None, blocks_mid, blocks_low]
    sources = [source_top[None], source_mid, source_low]
    sources = [jnp.swapaxes(source, 1, 2) for source in sources]
    outputs = sweep(inverses, couplings, sources, pivots, sizes, lists)
    outputs = [jnp.swapaxes(output, 1, 2) for output in outputs]
    return (outputs[0][0], outputs[1], outputs[2])


def solution(mesh):
    placed = (
        P("row", "col"),
        P(None, "row", "col"),
        P(None, "row", "col"),
        P(None, "col", "row"),
        P(None, "col", "row"),
        P("col", None),
        P(None, "col", None),
        P(None, "col", None),
        P("row"),
        P(None, "row"),
        P(None, "row"),
        P(),
        P(),
        P(),
        P(),
    )
    return jax.shard_map(
        local,
        mesh=mesh,
        in_specs=placed,
        out_specs=(P("col", None), P(None, "col", None), P(None, "col", None)),
        check_vma=False,
    )
```

```python
import jax
import jax.numpy as jnp
from jax import lax
from jax.experimental import pallas as pl
from jax.experimental.pallas import tpu as pltpu
from jax.sharding import PartitionSpec as P

BLOCK = 128
NEAR = 4
BF16 = jnp.bfloat16
F32 = jnp.float32
VMEM_SPEC = pl.BlockSpec(memory_space=pltpu.VMEM)
SMEM_SPEC = pl.BlockSpec(memory_space=pltpu.SMEM)


def near_groups():
    size = lax.axis_size("col")
    return [[z * NEAR + x for x in range(NEAR)] for z in range(size // NEAR)]


def far_groups():
    size = lax.axis_size("col")
    return [[z * NEAR + x for z in range(size // NEAR)] for x in range(NEAR)]


def swap_near(pieces):
    return lax.all_to_all(pieces, "col", 0, 0, axis_index_groups=near_groups(), tiled=True)


def gather_near(value):
    return lax.all_gather(value, "col", axis_index_groups=near_groups(), axis=0)


def copies_of(value, size):
    return jnp.broadcast_to(value.astype(BF16)[None], (size,) + value.shape)


def spread_far(value):
    groups = far_groups()
    copies = copies_of(value, len(groups[0]))
    return lax.all_to_all(copies, "col", 0, 0, axis_index_groups=groups, tiled=True)


def spread_row(value):
    return lax.all_to_all(copies_of(value, lax.axis_size("row")), "row", 0, 0, tiled=True)


def sum_far(partial):
    return jnp.sum(spread_far(partial).astype(F32), axis=0)


def sum_row(partial):
    return jnp.sum(spread_row(partial).astype(F32), axis=0)


def level_mask(sizes, count, start):
    index = start + jnp.arange(count, dtype=jnp.int32)
    return (index[None, :] < sizes[:, None]).astype(F32)[:, None, :]


def dot(a, b, dims):
    return lax.dot_general(a, b, (dims, ((), ())), preferred_element_type=F32)


def place_kernel(here, blocks, whole, source, mask, inverse, out):
    parents = source.shape[0]
    held = source.shape[2] // BLOCK
    listed = blocks.shape[1]
    first = here[0] * held
    for p in range(parents):
        parts = []
        for b in range(held):
            parts.append(source[p, :, b * BLOCK : (b + 1) * BLOCK])
        residual = jnp.concatenate(parts, axis=-1)
        scratch_free = residual
        for c in (2 * p, 2 * p + 1):
            placed = []
            for b in range(held):
                def find(k, carry, c=c, b=b):
                    at, found = carry
                    hit = blocks[c, k] == first + b
                    return jnp.where(hit, k, at), jnp.where(hit, 1, found)

                at, found = lax.fori_loop(0, listed, find, (0, 0), unroll=True)
                lane = pl.multiple_of((at % NEAR) * BLOCK, BLOCK)
                tile = whole[at // NEAR, c, :, pl.ds(lane, BLOCK)].astype(F32)
                placed.append(tile * found.astype(F32))
            scratch_free = scratch_free - jnp.concatenate(placed, axis=-1)
        operand = (scratch_free * mask[p]).astype(BF16)
        width = inverse.shape[3]
        total = None
        for x in range(NEAR):
            part = dot(operand[:, x * width : (x + 1) * width], inverse[x, p], ((1,), (1,)))
            total = part if total is None else total + part
        out[p] = total


def place_and_solve(blocks, whole, source, mask, inverse):
    parents, width, _ = source.shape
    here = (lax.axis_index("col") // NEAR).reshape(1)
    return pl.pallas_call(
        place_kernel,
        out_shape=jax.ShapeDtypeStruct((parents, width, inverse.shape[2]), F32),
        in_specs=[SMEM_SPEC, SMEM_SPEC] + [VMEM_SPEC] * 4,
        out_specs=VMEM_SPEC,
        compiler_params=pltpu.CompilerParams(vmem_limit_bytes=32 << 20),
    )(here, blocks, whole, source, mask, inverse)


def pick_kernel(here, blocks, whole, coupling, out):
    children = blocks.shape[0]
    held = whole.shape[3] // BLOCK
    for c in range(children):
        total = None
        for x in range(NEAR):
            block = blocks[c, here[0] * NEAR + x]
            lane = pl.multiple_of((block % held) * BLOCK, BLOCK)
            tile = whole[block // held, c // 2, :, pl.ds(lane, BLOCK)]
            part = dot(tile, coupling[x, c], ((1,), (0,)))
            total = part if total is None else total + part
        out[c] = total


def pick_and_carry(blocks, whole, coupling):
    here = (lax.axis_index("col") // NEAR).reshape(1)
    return pl.pallas_call(
        pick_kernel,
        out_shape=jax.ShapeDtypeStruct((blocks.shape[0], whole.shape[2], coupling.shape[3]), F32),
        in_specs=[SMEM_SPEC, SMEM_SPEC] + [VMEM_SPEC] * 2,
        out_specs=VMEM_SPEC,
        compiler_params=pltpu.CompilerParams(vmem_limit_bytes=32 << 20),
    )(here, blocks, whole, coupling)


def update_of(coupling, solved):
    solved = solved.astype(BF16)
    parts = [
        jnp.einsum("fuk,fck->fcu", coupling[x], solved, preferred_element_type=F32)
        for x in range(NEAR)
    ]
    return jnp.concatenate(parts, axis=-1)


def transposed(inverse, vector):
    vector = vector.astype(BF16)
    parts = [
        jnp.einsum("fij,fci->fcj", inverse[x], vector, preferred_element_type=F32)
        for x in range(NEAR)
    ]
    return jnp.concatenate(parts, axis=-1)


def halves(value):
    high = value.astype(BF16)
    return high, (value - high.astype(F32)).astype(BF16)


def by_near(value):
    return value.reshape(NEAR, value.shape[0] // NEAR, value.shape[1])


def local(
    inverse_top,
    inverse_mid,
    inverse_low,
    coupling_mid,
    coupling_low,
    source_top,
    source_mid,
    source_low,
    pivots_top,
    pivots_mid,
    pivots_low,
    sizes_mid,
    sizes_low,
    blocks_mid,
    blocks_low,
):
    row_at = lax.axis_index("row")
    col_at = lax.axis_index("col")
    far_at = col_at // NEAR
    rhs = source_top.shape[1]
    width = rhs // NEAR
    n0, n1, n2 = source_top.shape[0], source_mid.shape[1], source_low.shape[1]
    k1, k2 = inverse_mid.shape[1], inverse_low.shape[1]
    top = jnp.full((1,), inverse_top.shape[0] * lax.axis_size("row"), jnp.int32)

    coupling_low_near = gather_near(coupling_low)
    inverse_mid_near = gather_near(inverse_mid)
    coupling_mid_near = gather_near(coupling_mid)
    inverse_top_near = gather_near(inverse_top)[:, None]

    row_mask_mid = level_mask(sizes_mid, k1, row_at * k1)
    row_mask_low = level_mask(sizes_low, k2, row_at * k2)
    col_mask_low = level_mask(sizes_low, n2, col_at * n2)
    wide_mask_mid = level_mask(sizes_mid, NEAR * n1, far_at * NEAR * n1)
    wide_mask_top = level_mask(top, NEAR * n0, far_at * NEAR * n0)

    source = jnp.swapaxes(source_low, 1, 2) * col_mask_low
    partial = jnp.einsum(
        "fij,fcj->cfi", inverse_low, source.astype(BF16), preferred_element_type=F32
    ).reshape(rhs, -1)
    others = jnp.concatenate([source_mid[0].T, source_mid[1].T, source_top.T], axis=-1)
    message = jnp.concatenate([partial.astype(BF16), *halves(others)], axis=-1)
    got = swap_near(by_near(message)).astype(F32)
    size = partial.shape[1]
    partial = jnp.sum(got[:, :, :size], axis=0)
    others = got[:, :, size : size + others.shape[1]] + got[:, :, size + others.shape[1] :]
    parts = jnp.swapaxes(others, 0, 1)
    wide_source_mid = jnp.stack(
        [parts[:, :, f * n1 : (f + 1) * n1].reshape(width, NEAR * n1) for f in range(2)]
    )
    wide_source_top = parts[:, :, 2 * n1 :].reshape(1, width, NEAR * n0)
    solved = sum_far(jnp.swapaxes(partial.reshape(width, -1, k2), 0, 1)) * row_mask_low
    scaled_low = solved * pivots_low[:, None, :]

    whole = spread_far(sum_row(update_of(coupling_low_near, solved)))
    partial = place_and_solve(blocks_low, whole, wide_source_mid, wide_mask_mid, inverse_mid_near)
    solved = sum_far(partial) * row_mask_mid
    scaled_mid = solved * pivots_mid[:, None, :]

    whole = spread_far(sum_row(update_of(coupling_mid_near, solved)))
    partial = place_and_solve(blocks_mid, whole, wide_source_top, wide_mask_top, inverse_top_near)
    scaled = sum_far(partial) * pivots_top[None, None, :]

    solution_top = sum_row(transposed(inverse_top_near, scaled))
    partial = pick_and_carry(blocks_mid, spread_far(solution_top), coupling_mid_near)
    residual = (scaled_mid - sum_far(partial)) * row_mask_mid
    solution_mid = sum_row(transposed(inverse_mid_near, residual)) * wide_mask_mid
    partial = pick_and_carry(blocks_low, spread_far(solution_mid), coupling_low_near)
    residual = (scaled_low - sum_far(partial)) * row_mask_low

    upper = jnp.concatenate(
        [
            solution_top[0].reshape(width, NEAR, n0),
            solution_mid[0].reshape(width, NEAR, n1),
            solution_mid[1].reshape(width, NEAR, n1),
        ],
        axis=-1,
    )
    upper = jnp.concatenate(halves(upper), axis=-1)
    flat = jnp.swapaxes(residual, 0, 1).reshape(width, -1).astype(BF16)
    size = flat.shape[1]
    message = jnp.concatenate([copies_of(flat, NEAR), jnp.swapaxes(upper, 0, 1)], axis=-1)
    got = swap_near(message).reshape(rhs, -1)
    upper = got[:, size:].astype(F32)
    upper = upper[:, : upper.shape[1] // 2] + upper[:, upper.shape[1] // 2 :]
    residual = got[:, :size].reshape(rhs, -1, k2)
    partial = jnp.einsum("fij,cfi->fcj", inverse_low, residual, preferred_element_type=F32)
    solution_low = sum_row(partial) * col_mask_low
    return (
        upper[:, :n0].T,
        jnp.stack([upper[:, n0 : n0 + n1].T, upper[:, n0 + n1 :].T]),
        jnp.swapaxes(solution_low, 1, 2),
    )


def solution(mesh):
    placed = (
        P("row", "col"),
        P(None, "row", "col"),
        P(None, "row", "col"),
        P(None, "col", "row"),
        P(None, "col", "row"),
        P("col", None),
        P(None, "col", None),
        P(None, "col", None),
        P("row"),
        P(None, "row"),
        P(None, "row"),
        P(),
        P(),
        P(),
        P(),
    )
    return jax.shard_map(
        local,
        mesh=mesh,
        in_specs=placed,
        out_specs=(P("col", None), P(None, "col", None), P(None, "col", None)),
        check_vma=False,
    )
```

```python
import functools

import jax
import jax.numpy as jnp
from jax import lax
from jax.experimental import pallas as pl
from jax.experimental.pallas import tpu as pltpu
from jax.sharding import PartitionSpec as P

BLOCK = 128
NEAR = 4
BF16 = jnp.bfloat16
F32 = jnp.float32
VMEM_SPEC = pl.BlockSpec(memory_space=pltpu.VMEM)
SMEM_SPEC = pl.BlockSpec(memory_space=pltpu.SMEM)


def near_groups():
    size = lax.axis_size("col")
    return [[z * NEAR + x for x in range(NEAR)] for z in range(size // NEAR)]


def far_groups():
    size = lax.axis_size("col")
    return [[z * NEAR + x for z in range(size // NEAR)] for x in range(NEAR)]


def swap_near(pieces):
    return lax.all_to_all(pieces, "col", 0, 0, axis_index_groups=near_groups(), tiled=True)


def far_size():
    return lax.axis_size("col") // NEAR


def gather_near(value):
    size = lax.axis_size("col")
    parts = [value]
    for m in range(1, NEAR):
        parts.append(lax.ppermute(value, "col", [(i, i ^ m) for i in range(size)]))
    return parts


def gather_beside(value, message):
    value, message = lax.optimization_barrier((value, message))
    return gather_near(value), message


def xor_order(value):
    near = lax.axis_index("col") % NEAR
    for bit in (1, 2):
        swapped = jnp.stack([value[i ^ bit] for i in range(NEAR)])
        value = jnp.where((near & bit) != 0, swapped, value)
    return value


def copies_of(value, size):
    return jnp.broadcast_to(value.astype(BF16)[None], (size,) + value.shape)


def send_far(copies):
    groups = far_groups()
    return lax.all_to_all(copies, "col", 0, 0, axis_index_groups=groups, tiled=True)


def send_row(copies):
    return lax.all_to_all(copies, "row", 0, 0, tiled=True)


def level_mask_xor(sizes, count):
    near, far = lax.axis_index("col") % NEAR, lax.axis_index("col") // NEAR
    slots = near ^ jnp.arange(NEAR, dtype=jnp.int32)
    index = (far * NEAR + slots)[:, None] * count + jnp.arange(count, dtype=jnp.int32)
    return (index.reshape(1, -1) < sizes[:, None]).astype(F32)[:, None, :]


def update_table(blocks, held):
    near, far = lax.axis_index("col") % NEAR, lax.axis_index("col") // NEAR
    slots = near ^ jnp.arange(NEAR, dtype=jnp.int32)
    targets = (far * NEAR + slots)[:, None] * held + jnp.arange(held, dtype=jnp.int32)
    hits = (blocks[:, None, :] == targets.reshape(1, -1, 1)).astype(jnp.int32)
    return jnp.sum(hits * jnp.arange(1, blocks.shape[1] + 1, dtype=jnp.int32), axis=-1) - 1


def level_mask(sizes, count, start):
    index = start + jnp.arange(count, dtype=jnp.int32)
    return (index[None, :] < sizes[:, None]).astype(F32)[:, None, :]


def dot(a, b, dims):
    return lax.dot_general(a, b, (dims, ((), ())), preferred_element_type=F32)


def call(kernel, out_shape, scalars, arrays, **static):
    return pl.pallas_call(
        functools.partial(kernel, **static),
        out_shape=out_shape,
        in_specs=[SMEM_SPEC] * len(scalars) + [VMEM_SPEC] * len(arrays),
        out_specs=jax.tree.map(lambda _: VMEM_SPEC, out_shape),
        compiler_params=pltpu.CompilerParams(vmem_limit_bytes=16 << 20),
    )(*scalars, *arrays)


def arrived(parts, f):
    terms = [parts[i, f].astype(F32) for i in range(parts.shape[0])]
    while len(terms) > 1:
        terms = [terms[i] + terms[i + 1] for i in range(0, len(terms), 2)]
    return terms[0]


def write_copies(out, f, value):
    value = value.astype(BF16)
    for i in range(out.shape[0]):
        out[i, f] = value


def shape_of(*dims, dtype=BF16):
    return jax.ShapeDtypeStruct(dims, dtype)


def update_kernel(parts, mask, pivots, c0, c1, c2, c3, out, scaled):
    for f in range(parts.shape[1]):
        solved = arrived(parts, f) * mask[f]
        scaled[f] = solved * pivots[f]
        operand = solved.astype(BF16)
        update = [dot(operand, c[f], ((1,), (1,))) for c in (c0, c1, c2, c3)]
        write_copies(out, f, jnp.concatenate(update, axis=-1))


def update_of(parts, mask, pivots, couplings):
    _, fronts, width, count = parts.shape
    rows = lax.axis_size("row")
    out = (
        shape_of(rows, fronts, width, NEAR * couplings[0].shape[1]),
        shape_of(fronts, width, count, dtype=F32),
    )
    return call(update_kernel, out, [], [parts, mask, pivots[:, None, :], *couplings])


def relay_kernel(parts, out):
    for f in range(parts.shape[1]):
        write_copies(out, f, arrived(parts, f))


def relay(parts):
    return call(relay_kernel, shape_of(far_size(), *parts.shape[1:]), [], [parts])


def solved_kernel(parts, mask, out, solved):
    for f in range(parts.shape[1]):
        value = arrived(parts, f) * mask[f]
        solved[f] = value
        write_copies(out, f, value)


def relay_solved(parts, mask):
    shape = parts.shape[1:]
    out = (shape_of(far_size(), *shape), shape_of(*shape, dtype=F32))
    return call(solved_kernel, out, [], [parts, mask])


def place_kernel(here, table, whole, source, mask, i0, i1, i2, i3, out, *, base):
    near = here[1]
    n = i0.shape[2]
    held = n // BLOCK
    for p in range(i0.shape[0]):
        total = None
        for m, inverse in enumerate((i0, i1, i2, i3)):
            tiles = []
            for b in range(held):
                start = base + p * n + b * BLOCK
                tile = source[near ^ m, :, start : start + BLOCK]
                for c in (2 * p, 2 * p + 1):
                    at = table[c, m * held + b]
                    found = jnp.where(at >= 0, 1.0, 0.0).astype(F32)
                    at = jnp.maximum(at, 0)
                    lane = pl.multiple_of(((at % NEAR) ^ near) * BLOCK, BLOCK)
                    placed = whole[at // NEAR, c, :, pl.ds(lane, BLOCK)].astype(F32)
                    tile = tile - placed * found
                tiles.append(tile)
            operand = jnp.concatenate(tiles, axis=-1) * mask[p, :, m * n : (m + 1) * n]
            part = dot(operand.astype(BF16), inverse[p], ((1,), (1,)))
            total = part if total is None else total + part
        write_copies(out, p, total)


def place_and_solve(here, table, whole, source, mask, inverses, base):
    parents, count, _ = inverses[0].shape
    out = shape_of(far_size(), parents, whole.shape[2], count)
    arrays = [whole, source, mask, *inverses]
    return call(place_kernel, out, [here, table], arrays, base=base)


def root_kernel(parts, pivots, i0, i1, i2, i3, out):
    operand = (arrived(parts, 0) * pivots[...]).astype(BF16)
    pieces = [dot(operand, i[0], ((1,), (0,))) for i in (i0, i1, i2, i3)]
    write_copies(out, 0, jnp.concatenate(pieces, axis=-1))


def root_back(parts, pivots, inverses):
    out = shape_of(lax.axis_size("row"), 1, parts.shape[2], NEAR * inverses[0].shape[2])
    return call(root_kernel, out, [], [parts, pivots[None, :], *inverses])


def back_kernel(parts, scaled, mask, i0, i1, i2, i3, out):
    for p in range(parts.shape[1]):
        operand = ((scaled[p] - arrived(parts, p)) * mask[p]).astype(BF16)
        pieces = [dot(operand, i[p], ((1,), (0,))) for i in (i0, i1, i2, i3)]
        write_copies(out, p, jnp.concatenate(pieces, axis=-1))


def back(parts, scaled, mask, inverses):
    fronts, _, n = inverses[0].shape
    out = shape_of(lax.axis_size("row"), fronts, parts.shape[2], NEAR * n)
    return call(back_kernel, out, [], [parts, scaled, mask, *inverses])


def pick_kernel(here, blocks, whole, c0, c1, c2, c3, out):
    far, near = here[0], here[1]
    held = whole.shape[3] // BLOCK // NEAR
    for c in range(blocks.shape[0]):
        total = None
        for m, coupling in enumerate((c0, c1, c2, c3)):
            block = blocks[c, far * NEAR + (near ^ m)]
            owner = block // held
            slot = (owner % NEAR) ^ near
            lane = pl.multiple_of((slot * held + block % held) * BLOCK, BLOCK)
            tile = whole[owner // NEAR, c // 2, :, pl.ds(lane, BLOCK)]
            part = dot(tile, coupling[c], ((1,), (0,)))
            total = part if total is None else total + part
        write_copies(out, c, total)


def pick_and_carry(here, blocks, whole, couplings):
    children, _, count = couplings[0].shape
    out = shape_of(far_size(), children, whole.shape[2], count)
    return call(pick_kernel, out, [here, blocks], [whole, *couplings])


def halves(value):
    high = value.astype(BF16)
    return high, (value - high.astype(F32)).astype(BF16)


def by_near(value):
    return value.reshape(NEAR, value.shape[0] // NEAR, value.shape[1])


def local(
    inverse_top,
    inverse_mid,
    inverse_low,
    coupling_mid,
    coupling_low,
    source_top,
    source_mid,
    source_low,
    pivots_top,
    pivots_mid,
    pivots_low,
    sizes_mid,
    sizes_low,
    blocks_mid,
    blocks_low,
):
    row_at = lax.axis_index("row")
    col_at = lax.axis_index("col")
    far_at = col_at // NEAR
    rhs = source_top.shape[1]
    width = rhs // NEAR
    n0, n1, n2 = source_top.shape[0], source_mid.shape[1], source_low.shape[1]
    k1, k2 = inverse_mid.shape[1], inverse_low.shape[1]
    top = jnp.full((1,), inverse_top.shape[0] * lax.axis_size("row"), jnp.int32)

    here = jnp.stack([far_at, col_at % NEAR]).astype(jnp.int32)
    table_low = update_table(blocks_low, n1 // BLOCK)
    table_mid = update_table(blocks_mid, n0 // BLOCK)
    row_mask_mid = level_mask(sizes_mid, k1, row_at * k1)
    row_mask_low = level_mask(sizes_low, k2, row_at * k2)
    col_mask_low = level_mask(sizes_low, n2, col_at * n2)
    wide_mask_mid = level_mask_xor(sizes_mid, n1)
    wide_mask_top = level_mask_xor(top, n0)

    source = jnp.swapaxes(source_low, 1, 2) * col_mask_low
    partial = jnp.einsum(
        "fij,fcj->cfi", inverse_low, source.astype(BF16), preferred_element_type=F32
    ).reshape(rhs, -1)
    others = jnp.concatenate([source_mid[0].T, source_mid[1].T, source_top.T], axis=-1)
    message = jnp.concatenate([partial.astype(BF16), *halves(others)], axis=-1)
    coupling_low_near, message = gather_beside(coupling_low, message)
    got = swap_near(by_near(message)).astype(F32)
    size = partial.shape[1]
    partial = jnp.sum(got[:, :, :size], axis=0)
    others = got[:, :, size : size + others.shape[1]] + got[:, :, size + others.shape[1] :]
    partial = jnp.swapaxes(partial.reshape(width, -1, k2), 0, 1)
    inverse_mid_near, message = gather_beside(inverse_mid, copies_of(partial, far_size()))
    parts = send_far(message)

    message, scaled_low = update_of(parts, row_mask_low, pivots_low, coupling_low_near)
    coupling_mid_near, message = gather_beside(coupling_mid, message)
    message = relay(send_row(message))
    inverse_top_near, message = gather_beside(inverse_top[None], message)
    whole = send_far(message)
    parts = send_far(
        place_and_solve(here, table_low, whole, others, wide_mask_mid, inverse_mid_near, 0)
    )

    message, scaled_mid = update_of(parts, row_mask_mid, pivots_mid, coupling_mid_near)
    whole = send_far(relay(send_row(message)))
    parts = send_far(
        place_and_solve(here, table_mid, whole, others, wide_mask_top, inverse_top_near, 2 * n1)
    )

    message, solution_top = relay_solved(
        send_row(root_back(parts, pivots_top, inverse_top_near)), wide_mask_top
    )
    parts = send_far(pick_and_carry(here, blocks_mid, send_far(message), coupling_mid_near))
    message, solution_mid = relay_solved(
        send_row(back(parts, scaled_mid, row_mask_mid, inverse_mid_near)), wide_mask_mid
    )
    parts = send_far(pick_and_carry(here, blocks_low, send_far(message), coupling_low_near))
    residual = (scaled_low - jnp.sum(parts.astype(F32), axis=0)) * row_mask_low

    upper = jnp.concatenate(
        [
            solution_top[0].reshape(width, NEAR, n0),
            solution_mid[0].reshape(width, NEAR, n1),
            solution_mid[1].reshape(width, NEAR, n1),
        ],
        axis=-1,
    )
    upper = xor_order(jnp.swapaxes(jnp.concatenate(halves(upper), axis=-1), 0, 1))
    flat = jnp.swapaxes(residual, 0, 1).reshape(width, -1).astype(BF16)
    size = flat.shape[1]
    message = jnp.concatenate([copies_of(flat, NEAR), upper], axis=-1)
    got = swap_near(message).reshape(rhs, -1)
    upper = got[:, size:].astype(F32)
    upper = upper[:, : upper.shape[1] // 2] + upper[:, upper.shape[1] // 2 :]
    residual = got[:, :size].reshape(rhs, -1, k2)
    partial = jnp.einsum("fij,cfi->fcj", inverse_low, residual, preferred_element_type=F32)
    parts = send_row(copies_of(partial, lax.axis_size("row")))
    solution_low = jnp.sum(parts.astype(F32), axis=0) * col_mask_low
    return (
        upper[:, :n0].T,
        jnp.stack([upper[:, n0 : n0 + n1].T, upper[:, n0 + n1 :].T]),
        jnp.swapaxes(solution_low, 1, 2),
    )


def solution(mesh):
    placed = (
        P("row", "col"),
        P(None, "row", "col"),
        P(None, "row", "col"),
        P(None, "col", "row"),
        P(None, "col", "row"),
        P("col", None),
        P(None, "col", None),
        P(None, "col", None),
        P("row"),
        P(None, "row"),
        P(None, "row"),
        P(),
        P(),
        P(),
        P(),
    )
    return jax.shard_map(
        local,
        mesh=mesh,
        in_specs=placed,
        out_specs=(P("col", None), P(None, "col", None), P(None, "col", None)),
        check_vma=False,
    )
```

```python
import functools

import jax
import jax.numpy as jnp
from jax import lax
from jax.experimental import pallas as pl
from jax.experimental.pallas import tpu as pltpu
from jax.sharding import PartitionSpec as P

BLOCK = 128
NEAR = 4
BF16 = jnp.bfloat16
F32 = jnp.float32
VMEM_SPEC = pl.BlockSpec(memory_space=pltpu.VMEM)
SMEM_SPEC = pl.BlockSpec(memory_space=pltpu.SMEM)


def near_groups():
    size = lax.axis_size("col")
    return [[z * NEAR + x for x in range(NEAR)] for z in range(size // NEAR)]


def far_groups():
    size = lax.axis_size("col")
    return [[z * NEAR + x for z in range(size // NEAR)] for x in range(NEAR)]


def swap_near(pieces):
    return lax.all_to_all(pieces, "col", 0, 0, axis_index_groups=near_groups(), tiled=True)


def far_size():
    return lax.axis_size("col") // NEAR


def gather_near(value):
    return lax.all_gather(value, "col", axis_index_groups=near_groups(), axis=0)


def copies_of(value, size):
    return jnp.broadcast_to(value.astype(BF16)[None], (size,) + value.shape)


def send_far(copies):
    groups = far_groups()
    return lax.all_to_all(copies, "col", 0, 0, axis_index_groups=groups, tiled=True)


def send_row(copies):
    return lax.all_to_all(copies, "row", 0, 0, tiled=True)


def update_table(blocks, far_at, held):
    targets = far_at * NEAR * held + jnp.arange(NEAR * held, dtype=jnp.int32)
    hits = (blocks[:, None, :] == targets[None, :, None]).astype(jnp.int32)
    return jnp.sum(hits * jnp.arange(1, blocks.shape[1] + 1, dtype=jnp.int32), axis=-1) - 1


def send_col(copies):
    return lax.all_to_all(copies, "col", 0, 0, tiled=True)


def level_mask(sizes, count, start):
    index = start + jnp.arange(count, dtype=jnp.int32)
    return (index[None, :] < sizes[:, None]).astype(F32)[:, None, :]


def dot(a, b, dims):
    return lax.dot_general(a, b, (dims, ((), ())), preferred_element_type=F32)


def call(kernel, out_shape, scalars, arrays, **static):
    return pl.pallas_call(
        functools.partial(kernel, **static),
        out_shape=out_shape,
        in_specs=[SMEM_SPEC] * len(scalars) + [VMEM_SPEC] * len(arrays),
        out_specs=jax.tree.map(lambda _: VMEM_SPEC, out_shape),
        compiler_params=pltpu.CompilerParams(vmem_limit_bytes=16 << 20),
    )(*scalars, *arrays)


def arrived(parts, f):
    terms = [parts[i, f].astype(F32) for i in range(parts.shape[0])]
    while len(terms) > 1:
        terms = [terms[i] + terms[i + 1] for i in range(0, len(terms), 2)]
    return terms[0]


def write_copies(out, f, value):
    value = value.astype(BF16)
    for i in range(out.shape[0]):
        out[i, f] = value


def shape_of(*dims, dtype=BF16):
    return jax.ShapeDtypeStruct(dims, dtype)


def first_kernel(parts, mask, pivots, out, scaled):
    for f in range(parts.shape[1]):
        solved = arrived(parts, f) * mask[f]
        scaled[f] = solved * pivots[f]
        write_copies(out, f, solved)


def first_solved(parts, mask, pivots):
    shape = parts.shape[1:]
    out = (shape_of(NEAR, *shape), shape_of(*shape, dtype=F32))
    return call(first_kernel, out, [], [parts, mask, pivots[:, None, :]])


def first_update_kernel(parts, coupling, out):
    for f in range(coupling.shape[0]):
        pieces = [parts[x, f].astype(F32) for x in range(NEAR)]
        operand = jnp.concatenate(pieces, axis=0).astype(BF16)
        write_copies(out, f, dot(operand, coupling[f], ((1,), (1,))))


def first_update(parts, coupling):
    fronts, count, _ = coupling.shape
    out = shape_of(lax.axis_size("row"), fronts, NEAR * parts.shape[2], count)
    return call(first_update_kernel, out, [], [parts, coupling])


def scatter_kernel(parts, out):
    width = out.shape[2]
    for f in range(parts.shape[1]):
        value = arrived(parts, f)
        for x in range(NEAR):
            share = value[x * width : (x + 1) * width].astype(BF16)
            for z in range(out.shape[0] // NEAR):
                out[z * NEAR + x, f] = share


def relay_scattered(parts):
    _, fronts, rhs, count = parts.shape
    out = shape_of(lax.axis_size("col"), fronts, rhs // NEAR, count)
    return call(scatter_kernel, out, [], [parts])


def update_kernel(parts, mask, pivots, coupling, out, scaled):
    for f in range(parts.shape[1]):
        solved = arrived(parts, f) * mask[f]
        scaled[f] = solved * pivots[f]
        operand = solved.astype(BF16)
        update = [dot(operand, coupling[x, f], ((1,), (1,))) for x in range(NEAR)]
        write_copies(out, f, jnp.concatenate(update, axis=-1))


def update_of(parts, mask, pivots, coupling):
    _, fronts, width, count = parts.shape
    rows = lax.axis_size("row")
    out = (
        shape_of(rows, fronts, width, NEAR * coupling.shape[2]),
        shape_of(fronts, width, count, dtype=F32),
    )
    return call(update_kernel, out, [], [parts, mask, pivots[:, None, :], coupling])


def relay_kernel(parts, out):
    for f in range(parts.shape[1]):
        write_copies(out, f, arrived(parts, f))


def relay(parts):
    return call(relay_kernel, shape_of(far_size(), *parts.shape[1:]), [], [parts])


def solved_kernel(parts, mask, out, solved):
    for f in range(parts.shape[1]):
        value = arrived(parts, f) * mask[f]
        solved[f] = value
        write_copies(out, f, value)


def relay_solved(parts, mask):
    shape = parts.shape[1:]
    out = (shape_of(far_size(), *shape), shape_of(*shape, dtype=F32))
    return call(solved_kernel, out, [], [parts, mask])


def place_kernel(table, whole, source, mask, inverse, out, *, base):
    n = inverse.shape[2]
    held = n // BLOCK
    count = out.shape[3]
    spread = whole.shape[3] // BLOCK
    for p in range(out.shape[1]):
        total = None
        for x in range(NEAR):
            tiles = []
            for b in range(held):
                start = base + p * n + b * BLOCK
                tile = source[x, :, start : start + BLOCK]
                for c in (2 * p, 2 * p + 1):
                    at = table[c, x * held + b]
                    found = jnp.where(at >= 0, 1.0, 0.0).astype(F32)
                    at = jnp.maximum(at, 0)
                    if spread == 1:
                        placed = whole[at, c]
                    else:
                        lane = pl.multiple_of((at % spread) * BLOCK, BLOCK)
                        placed = whole[at // spread, c, :, pl.ds(lane, BLOCK)]
                    tile = tile - placed.astype(F32) * found
                tiles.append(tile)
            operand = jnp.concatenate(tiles, axis=-1) * mask[p, :, x * n : (x + 1) * n]
            rows = inverse[x, p * count : (p + 1) * count]
            part = dot(operand.astype(BF16), rows, ((1,), (1,)))
            total = part if total is None else total + part
        write_copies(out, p, total)


def place_and_solve(table, whole, source, mask, inverse, parents, count, base):
    out = shape_of(far_size(), parents, whole.shape[2], count)
    return call(place_kernel, out, [table], [whole, source, mask, inverse], base=base)


def root_kernel(parts, pivots, inverse, out):
    operand = (arrived(parts, 0) * pivots[...]).astype(BF16)
    pieces = [dot(operand, inverse[x], ((1,), (0,))) for x in range(NEAR)]
    write_copies(out, 0, jnp.concatenate(pieces, axis=-1))


def root_back(parts, pivots, inverse):
    out = shape_of(lax.axis_size("row"), 1, parts.shape[2], NEAR * inverse.shape[2])
    return call(root_kernel, out, [], [parts, pivots[None, :], inverse])


def back_kernel(parts, scaled, mask, inverse, out):
    count = parts.shape[3]
    for p in range(parts.shape[1]):
        operand = ((scaled[p] - arrived(parts, p)) * mask[p]).astype(BF16)
        pieces = [
            dot(operand, inverse[x, p * count : (p + 1) * count], ((1,), (0,)))
            for x in range(NEAR)
        ]
        write_copies(out, p, jnp.concatenate(pieces, axis=-1))


def back(parts, scaled, mask, inverse):
    _, fronts, width, _ = parts.shape
    out = shape_of(lax.axis_size("row"), fronts, width, NEAR * inverse.shape[2])
    return call(back_kernel, out, [], [parts, scaled, mask, inverse])


def pick_kernel(far, blocks, whole, coupling, out):
    held = whole.shape[3] // BLOCK
    for c in range(blocks.shape[0]):
        total = None
        for x in range(NEAR):
            block = blocks[c, far[0] * NEAR + x]
            lane = pl.multiple_of((block % held) * BLOCK, BLOCK)
            tile = whole[block // held, c // 2, :, pl.ds(lane, BLOCK)]
            part = dot(tile, coupling[x, c], ((1,), (0,)))
            total = part if total is None else total + part
        write_copies(out, c, total)


def pick_and_carry(far, blocks, whole, coupling):
    _, children, _, count = coupling.shape
    out = shape_of(far_size(), children, whole.shape[2], count)
    return call(pick_kernel, out, [far, blocks], [whole, coupling])


def halves(value):
    high = value.astype(BF16)
    return high, (value - high.astype(F32)).astype(BF16)


def by_near(value):
    return value.reshape(NEAR, value.shape[0] // NEAR, value.shape[1])


def local(
    inverse_top,
    inverse_mid,
    inverse_low,
    coupling_mid,
    coupling_low,
    source_top,
    source_mid,
    source_low,
    pivots_top,
    pivots_mid,
    pivots_low,
    sizes_mid,
    sizes_low,
    blocks_mid,
    blocks_low,
):
    row_at = lax.axis_index("row")
    col_at = lax.axis_index("col")
    far_at = col_at // NEAR
    rhs = source_top.shape[1]
    width = rhs // NEAR
    n0, n1, n2 = source_top.shape[0], source_mid.shape[1], source_low.shape[1]
    k1, k2 = inverse_mid.shape[1], inverse_low.shape[1]
    top = jnp.full((1,), inverse_top.shape[0] * lax.axis_size("row"), jnp.int32)

    others = jnp.concatenate([source_mid[0].T, source_mid[1].T, source_top.T], axis=-1)
    halved = jnp.concatenate(halves(others), axis=-1).reshape(-1, n1)
    packed = jnp.concatenate([inverse_mid.reshape(-1, n1), halved], axis=0)
    packed, coupling_mid = lax.optimization_barrier((packed, coupling_mid))
    packed_near = gather_near(packed)
    coupling_mid_near = gather_near(coupling_mid)
    inverse_top_near = gather_near(inverse_top)
    coupling_low_near = gather_near(coupling_low)

    far = far_at.reshape(1)
    table_low = update_table(blocks_low, far_at, n1 // BLOCK)
    table_mid = update_table(blocks_mid, far_at, n0 // BLOCK)
    row_mask_mid = level_mask(sizes_mid, k1, row_at * k1)
    row_mask_low = level_mask(sizes_low, k2, row_at * k2)
    col_mask_low = level_mask(sizes_low, n2, col_at * n2)
    wide_mask_mid = level_mask(sizes_mid, NEAR * n1, far_at * NEAR * n1)
    wide_mask_top = level_mask(top, NEAR * n0, far_at * NEAR * n0)

    source = jnp.swapaxes(source_low, 1, 2) * col_mask_low
    partial = jnp.einsum(
        "fij,fcj->cfi", inverse_low, source.astype(BF16), preferred_element_type=F32
    ).reshape(rhs, -1)
    got = swap_near(by_near(partial.astype(BF16))).astype(F32)
    partial = jnp.swapaxes(jnp.sum(got, axis=0).reshape(width, -1, k2), 0, 1)
    parts = send_far(copies_of(partial, far_size()))
    message, scaled_low = first_solved(parts, row_mask_low, pivots_low)
    message = first_update(swap_near(message), coupling_low)
    whole = send_col(relay_scattered(send_row(message)))

    halved = packed_near[:, 2 * k1 :].reshape(NEAR, rhs, -1)
    halved = lax.dynamic_slice_in_dim(halved, (col_at % NEAR) * width, width, 1).astype(F32)
    size = halved.shape[2] // 2
    others = halved[:, :, :size] + halved[:, :, size:]
    parts = send_far(
        place_and_solve(table_low, whole, others, wide_mask_mid, packed_near, 2, k1, 0)
    )

    message, scaled_mid = update_of(parts, row_mask_mid, pivots_mid, coupling_mid_near)
    whole = send_far(relay(send_row(message)))
    k0 = inverse_top.shape[0]
    parts = send_far(
        place_and_solve(table_mid, whole, others, wide_mask_top, inverse_top_near, 1, k0, 2 * n1)
    )

    message, solution_top = relay_solved(
        send_row(root_back(parts, pivots_top, inverse_top_near)), wide_mask_top
    )
    parts = send_far(pick_and_carry(far, blocks_mid, send_far(message), coupling_mid_near))
    message, solution_mid = relay_solved(
        send_row(back(parts, scaled_mid, row_mask_mid, packed_near)), wide_mask_mid
    )
    parts = send_far(pick_and_carry(far, blocks_low, send_far(message), coupling_low_near))
    residual = (scaled_low - jnp.sum(parts.astype(F32), axis=0)) * row_mask_low

    upper = jnp.concatenate(
        [
            solution_top[0].reshape(width, NEAR, n0),
            solution_mid[0].reshape(width, NEAR, n1),
            solution_mid[1].reshape(width, NEAR, n1),
        ],
        axis=-1,
    )
    upper = jnp.swapaxes(jnp.concatenate(halves(upper), axis=-1), 0, 1)
    flat = jnp.swapaxes(residual, 0, 1).reshape(width, -1).astype(BF16)
    size = flat.shape[1]
    message = jnp.concatenate([copies_of(flat, NEAR), upper], axis=-1)
    got = swap_near(message).reshape(rhs, -1)
    upper = got[:, size:].astype(F32)
    upper = upper[:, : upper.shape[1] // 2] + upper[:, upper.shape[1] // 2 :]
    residual = got[:, :size].reshape(rhs, -1, k2)
    partial = jnp.einsum("fij,cfi->fcj", inverse_low, residual, preferred_element_type=F32)
    parts = send_row(copies_of(partial, lax.axis_size("row")))
    solution_low = jnp.sum(parts.astype(F32), axis=0) * col_mask_low
    return (
        upper[:, :n0].T,
        jnp.stack([upper[:, n0 : n0 + n1].T, upper[:, n0 + n1 :].T]),
        jnp.swapaxes(solution_low, 1, 2),
    )


def solution(mesh):
    placed = (
        P("row", "col"),
        P(None, "row", "col"),
        P(None, "row", "col"),
        P(None, "col", "row"),
        P(None, "col", "row"),
        P("col", None),
        P(None, "col", None),
        P(None, "col", None),
        P("row"),
        P(None, "row"),
        P(None, "row"),
        P(),
        P(),
        P(),
        P(),
    )
    return jax.shard_map(
        local,
        mesh=mesh,
        in_specs=placed,
        out_specs=(P("col", None), P(None, "col", None), P(None, "col", None)),
        check_vma=False,
    )
```

```python
import functools

import jax
import jax.numpy as jnp
from jax import lax
from jax.experimental import pallas as pl
from jax.experimental.pallas import tpu as pltpu
from jax.sharding import PartitionSpec as P

BLOCK = 128
NEAR = 4
BF16 = jnp.bfloat16
F32 = jnp.float32
VMEM_SPEC = pl.BlockSpec(memory_space=pltpu.VMEM)
SMEM_SPEC = pl.BlockSpec(memory_space=pltpu.SMEM)


def near_groups():
    size = lax.axis_size("col")
    return [[z * NEAR + x for x in range(NEAR)] for z in range(size // NEAR)]


def far_groups():
    size = lax.axis_size("col")
    return [[z * NEAR + x for z in range(size // NEAR)] for x in range(NEAR)]


def swap_near(pieces):
    return lax.all_to_all(pieces, "col", 0, 0, axis_index_groups=near_groups(), tiled=True)


def far_size():
    return lax.axis_size("col") // NEAR


def gather_near(value):
    return lax.all_gather(value, "col", axis_index_groups=near_groups(), axis=0)


def copies_of(value, size):
    return jnp.broadcast_to(value.astype(BF16)[None], (size,) + value.shape)


def send_far(copies):
    groups = far_groups()
    return lax.all_to_all(copies, "col", 0, 0, axis_index_groups=groups, tiled=True)


def send_row(copies):
    return lax.all_to_all(copies, "row", 0, 0, tiled=True)


def update_table(blocks, far_at, held):
    targets = far_at * NEAR * held + jnp.arange(NEAR * held, dtype=jnp.int32)
    hits = (blocks[:, None, :] == targets[None, :, None]).astype(jnp.int32)
    return jnp.sum(hits * jnp.arange(1, blocks.shape[1] + 1, dtype=jnp.int32), axis=-1) - 1


def send_col(copies):
    return lax.all_to_all(copies, "col", 0, 0, tiled=True)


def level_mask(sizes, count, start):
    index = start + jnp.arange(count, dtype=jnp.int32)
    return (index[None, :] < sizes[:, None]).astype(F32)[:, None, :]


def dot(a, b, dims):
    return lax.dot_general(a, b, (dims, ((), ())), preferred_element_type=F32)


def call(kernel, out_shape, scalars, arrays, fetched=(), **static):
    specs = [SMEM_SPEC] * len(scalars) + [VMEM_SPEC] * len(arrays)
    specs += [pl.BlockSpec(memory_space=pl.ANY)] * len(fetched)
    scratch = []
    for array in fetched:
        scratch += [pltpu.VMEM(array.shape, array.dtype), pltpu.SemaphoreType.DMA((array.shape[0],))]
    return pl.pallas_call(
        functools.partial(kernel, **static),
        out_shape=out_shape,
        in_specs=specs,
        out_specs=jax.tree.map(lambda _: VMEM_SPEC, out_shape),
        scratch_shapes=scratch,
        compiler_params=pltpu.CompilerParams(vmem_limit_bytes=16 << 20),
    )(*scalars, *arrays, *fetched)


def fetch(array, held, semaphores):
    pieces = [
        pltpu.make_async_copy(array.at[x], held.at[x], semaphores.at[x])
        for x in range(array.shape[0])
    ]
    for piece in pieces:
        piece.start()
    return pieces


def arrived(parts, f):
    terms = [parts[i, f].astype(F32) for i in range(parts.shape[0])]
    while len(terms) > 1:
        terms = [terms[i] + terms[i + 1] for i in range(0, len(terms), 2)]
    return terms[0]


def write_copies(out, f, value):
    value = value.astype(BF16)
    for i in range(out.shape[0]):
        out[i, f] = value


def shape_of(*dims, dtype=BF16):
    return jax.ShapeDtypeStruct(dims, dtype)


def total_kernel(parts, out):
    terms = [parts[i].astype(F32) for i in range(parts.shape[0])]
    while len(terms) > 1:
        terms = [terms[i] + terms[i + 1] for i in range(0, len(terms), 2)]
    value = terms[0].astype(BF16)
    for i in range(out.shape[0]):
        out[i] = value


def relay_pieces(parts):
    return call(total_kernel, shape_of(*parts.shape), [], [parts])


def first_update_kernel(near, parts, mask, pivots, coupling, out, scaled):
    fronts = coupling.shape[0]
    pieces = parts.shape[0] // fronts
    share = pieces // NEAR
    for f in range(fronts):
        solved = [parts[f * pieces + g].astype(F32) for g in range(pieces)]
        operand = (jnp.concatenate(solved, axis=0) * mask[f]).astype(BF16)
        write_copies(out, f, dot(operand, coupling[f], ((1,), (1,))))
        first = f * pieces + near[0] * share
        solved = [parts[first + g].astype(F32) for g in range(share)]
        scaled[f] = jnp.concatenate(solved, axis=0) * mask[f] * pivots[f]


def first_update(near, parts, mask, pivots, coupling):
    fronts, count, solved = coupling.shape
    rhs = parts.shape[0] * parts.shape[1] // fronts
    out = (
        shape_of(lax.axis_size("row"), fronts, rhs, count),
        shape_of(fronts, rhs // NEAR, solved, dtype=F32),
    )
    return call(first_update_kernel, out, [near], [parts, mask, pivots[:, None, :], coupling])


def last_kernel(got, inverse, out):
    count = inverse.shape[1]
    for f in range(inverse.shape[0]):
        pieces = [got[x, :, f * count : (f + 1) * count].astype(F32) for x in range(NEAR)]
        operand = jnp.concatenate(pieces, axis=0).astype(BF16)
        write_copies(out, f, dot(operand, inverse[f], ((1,), (0,))))


def last_product(got, inverse):
    fronts, _, n = inverse.shape
    out = shape_of(lax.axis_size("row"), fronts, NEAR * got.shape[1], n)
    return call(last_kernel, out, [], [got, inverse])


def scatter_kernel(parts, out):
    width = out.shape[2]
    for f in range(parts.shape[1]):
        value = arrived(parts, f)
        for x in range(NEAR):
            share = value[x * width : (x + 1) * width].astype(BF16)
            for z in range(out.shape[0] // NEAR):
                out[z * NEAR + x, f] = share


def relay_scattered(parts):
    _, fronts, rhs, count = parts.shape
    out = shape_of(lax.axis_size("col"), fronts, rhs // NEAR, count)
    return call(scatter_kernel, out, [], [parts])


def update_kernel(parts, mask, pivots, coupling, out, scaled):
    for f in range(parts.shape[1]):
        solved = arrived(parts, f) * mask[f]
        scaled[f] = solved * pivots[f]
        operand = solved.astype(BF16)
        update = [dot(operand, coupling[x, f], ((1,), (1,))) for x in range(NEAR)]
        write_copies(out, f, jnp.concatenate(update, axis=-1))


def update_of(parts, mask, pivots, coupling):
    _, fronts, width, count = parts.shape
    rows = lax.axis_size("row")
    out = (
        shape_of(rows, fronts, width, NEAR * coupling.shape[2]),
        shape_of(fronts, width, count, dtype=F32),
    )
    return call(update_kernel, out, [], [parts, mask, pivots[:, None, :], coupling])


def relay_kernel(parts, out):
    for f in range(parts.shape[1]):
        write_copies(out, f, arrived(parts, f))


def relay(parts):
    return call(relay_kernel, shape_of(far_size(), *parts.shape[1:]), [], [parts])


def solved_kernel(parts, mask, out, solved):
    for f in range(parts.shape[1]):
        value = arrived(parts, f) * mask[f]
        solved[f] = value
        write_copies(out, f, value)


def relay_solved(parts, mask):
    shape = parts.shape[1:]
    out = (shape_of(far_size(), *shape), shape_of(*shape, dtype=F32))
    return call(solved_kernel, out, [], [parts, mask])


def place_kernel(table, whole, source, mask, inverse_at, out, inverse, semaphores, *, base):
    copies = fetch(inverse_at, inverse, semaphores)
    n = inverse.shape[2]
    held = n // BLOCK
    count = out.shape[3]
    spread = whole.shape[3] // BLOCK
    for p in range(out.shape[1]):
        total = None
        for x in range(NEAR):
            tiles = []
            for b in range(held):
                start = base + p * n + b * BLOCK
                tile = source[x, :, start : start + BLOCK]
                for c in (2 * p, 2 * p + 1):
                    at = table[c, x * held + b]
                    found = jnp.where(at >= 0, 1.0, 0.0).astype(F32)
                    at = jnp.maximum(at, 0)
                    if spread == 1:
                        placed = whole[at, c]
                    else:
                        lane = pl.multiple_of((at % spread) * BLOCK, BLOCK)
                        placed = whole[at // spread, c, :, pl.ds(lane, BLOCK)]
                    tile = tile - placed.astype(F32) * found
                tiles.append(tile)
            operand = jnp.concatenate(tiles, axis=-1) * mask[p, :, x * n : (x + 1) * n]
            if p == 0:
                copies[x].wait()
            rows = inverse[x, p * count : (p + 1) * count]
            part = dot(operand.astype(BF16), rows, ((1,), (1,)))
            total = part if total is None else total + part
        write_copies(out, p, total)


def place_and_solve(table, whole, source, mask, inverse, parents, count, base):
    out = shape_of(far_size(), parents, whole.shape[2], count)
    return call(place_kernel, out, [table], [whole, source, mask], [inverse], base=base)


def root_kernel(parts, pivots, inverse_at, out, inverse, semaphores):
    copies = fetch(inverse_at, inverse, semaphores)
    operand = (arrived(parts, 0) * pivots[...]).astype(BF16)
    pieces = []
    for x in range(NEAR):
        copies[x].wait()
        pieces.append(dot(operand, inverse[x], ((1,), (0,))))
    write_copies(out, 0, jnp.concatenate(pieces, axis=-1))


def root_back(parts, pivots, inverse):
    out = shape_of(lax.axis_size("row"), 1, parts.shape[2], NEAR * inverse.shape[2])
    return call(root_kernel, out, [], [parts, pivots[None, :]], [inverse])


def back_kernel(parts, scaled, mask, inverse, out):
    count = parts.shape[3]
    for p in range(parts.shape[1]):
        operand = ((scaled[p] - arrived(parts, p)) * mask[p]).astype(BF16)
        pieces = [
            dot(operand, inverse[x, p * count : (p + 1) * count], ((1,), (0,)))
            for x in range(NEAR)
        ]
        write_copies(out, p, jnp.concatenate(pieces, axis=-1))


def back(parts, scaled, mask, inverse):
    _, fronts, width, _ = parts.shape
    out = shape_of(lax.axis_size("row"), fronts, width, NEAR * inverse.shape[2])
    return call(back_kernel, out, [], [parts, scaled, mask, inverse])


def pick_kernel(far, blocks, whole, coupling, out):
    held = whole.shape[3] // BLOCK
    for c in range(blocks.shape[0]):
        total = None
        for x in range(NEAR):
            block = blocks[c, far[0] * NEAR + x]
            lane = pl.multiple_of((block % held) * BLOCK, BLOCK)
            tile = whole[block // held, c // 2, :, pl.ds(lane, BLOCK)]
            part = dot(tile, coupling[x, c], ((1,), (0,)))
            total = part if total is None else total + part
        write_copies(out, c, total)


def pick_and_carry(far, blocks, whole, coupling):
    _, children, _, count = coupling.shape
    out = shape_of(far_size(), children, whole.shape[2], count)
    return call(pick_kernel, out, [far, blocks], [whole, coupling])


def halves(value):
    high = value.astype(BF16)
    return high, (value - high.astype(F32)).astype(BF16)


def local(
    inverse_top,
    inverse_mid,
    inverse_low,
    coupling_mid,
    coupling_low,
    source_top,
    source_mid,
    source_low,
    pivots_top,
    pivots_mid,
    pivots_low,
    sizes_mid,
    sizes_low,
    blocks_mid,
    blocks_low,
):
    row_at = lax.axis_index("row")
    col_at = lax.axis_index("col")
    far_at = col_at // NEAR
    rhs = source_top.shape[1]
    width = rhs // NEAR
    n0, n1, n2 = source_top.shape[0], source_mid.shape[1], source_low.shape[1]
    k1, k2 = inverse_mid.shape[1], inverse_low.shape[1]
    top = jnp.full((1,), inverse_top.shape[0] * lax.axis_size("row"), jnp.int32)

    far, near = far_at.reshape(1), (col_at % NEAR).reshape(1)
    table_low = update_table(blocks_low, far_at, n1 // BLOCK)
    table_mid = update_table(blocks_mid, far_at, n0 // BLOCK)
    row_mask_mid = level_mask(sizes_mid, k1, row_at * k1)
    row_mask_low = level_mask(sizes_low, k2, row_at * k2)
    col_mask_low = level_mask(sizes_low, n2, col_at * n2)
    wide_mask_mid = level_mask(sizes_mid, NEAR * n1, far_at * NEAR * n1)
    wide_mask_top = level_mask(top, NEAR * n0, far_at * NEAR * n0)

    source = jnp.swapaxes(source_low, 1, 2) * col_mask_low
    partial = jnp.einsum(
        "fij,fcj->fci", inverse_low, source.astype(BF16), preferred_element_type=F32
    )
    message = partial.astype(BF16).reshape(lax.axis_size("col"), -1, k2)

    coupling_mid_near = gather_near(coupling_mid)
    inverse_mid, source_mid, source_top, message = lax.optimization_barrier(
        (inverse_mid, source_mid, source_top, message)
    )
    others = jnp.concatenate([source_mid[0].T, source_mid[1].T, source_top.T], axis=-1)
    halved = jnp.concatenate(halves(others), axis=-1).reshape(-1, n1)
    packed = jnp.concatenate([inverse_mid.reshape(-1, n1), halved], axis=0)
    packed, inverse_top, coupling_low_late = lax.optimization_barrier(
        (packed, inverse_top, coupling_low)
    )
    packed_near = gather_near(packed)
    inverse_top_near = gather_near(inverse_top)
    coupling_low_near = gather_near(coupling_low_late)

    parts = send_col(relay_pieces(send_col(message)))
    message, scaled_low = first_update(near, parts, row_mask_low, pivots_low, coupling_low)
    whole = send_col(relay_scattered(send_row(message)))

    halved = packed_near[:, 2 * k1 :].reshape(NEAR, rhs, -1)
    halved = lax.dynamic_slice_in_dim(halved, (col_at % NEAR) * width, width, 1).astype(F32)
    size = halved.shape[2] // 2
    others = halved[:, :, :size] + halved[:, :, size:]
    message = place_and_solve(table_low, whole, others, wide_mask_mid, packed_near, 2, k1, 0)
    coupling_mid_near, message = lax.optimization_barrier((coupling_mid_near, message))
    parts = send_far(message)

    message, scaled_mid = update_of(parts, row_mask_mid, pivots_mid, coupling_mid_near)
    whole = send_far(relay(send_row(message)))
    k0 = inverse_top.shape[0]
    parts = send_far(
        place_and_solve(table_mid, whole, others, wide_mask_top, inverse_top_near, 1, k0, 2 * n1)
    )

    message, solution_top = relay_solved(
        send_row(root_back(parts, pivots_top, inverse_top_near)), wide_mask_top
    )
    message = pick_and_carry(far, blocks_mid, send_far(message), coupling_mid_near)
    coupling_low_near, message = lax.optimization_barrier((coupling_low_near, message))
    parts = send_far(message)
    message, solution_mid = relay_solved(
        send_row(back(parts, scaled_mid, row_mask_mid, packed_near)), wide_mask_mid
    )
    parts = send_far(pick_and_carry(far, blocks_low, send_far(message), coupling_low_near))
    residual = (scaled_low - jnp.sum(parts.astype(F32), axis=0)) * row_mask_low

    upper = jnp.concatenate(
        [
            solution_top[0].reshape(width, NEAR, n0),
            solution_mid[0].reshape(width, NEAR, n1),
            solution_mid[1].reshape(width, NEAR, n1),
        ],
        axis=-1,
    )
    upper = jnp.swapaxes(jnp.concatenate(halves(upper), axis=-1), 0, 1)
    flat = jnp.swapaxes(residual, 0, 1).reshape(width, -1).astype(BF16)
    size = flat.shape[1]
    message = jnp.concatenate([copies_of(flat, NEAR), upper], axis=-1)
    got = swap_near(message)
    parts = send_row(last_product(got, inverse_low))
    upper = got[:, :, size:].astype(F32).reshape(rhs, -1)
    upper = upper[:, : upper.shape[1] // 2] + upper[:, upper.shape[1] // 2 :]
    solution_low = jnp.sum(parts.astype(F32), axis=0) * col_mask_low
    return (
        upper[:, :n0].T,
        jnp.stack([upper[:, n0 : n0 + n1].T, upper[:, n0 + n1 :].T]),
        jnp.swapaxes(solution_low, 1, 2),
    )


def solution(mesh):
    placed = (
        P("row", "col"),
        P(None, "row", "col"),
        P(None, "row", "col"),
        P(None, "col", "row"),
        P(None, "col", "row"),
        P("col", None),
        P(None, "col", None),
        P(None, "col", None),
        P("row"),
        P(None, "row"),
        P(None, "row"),
        P(),
        P(),
        P(),
        P(),
    )
    return jax.shard_map(
        local,
        mesh=mesh,
        in_specs=placed,
        out_specs=(P("col", None), P(None, "col", None), P(None, "col", None)),
        check_vma=False,
    )
```

```python
import functools

import jax
import jax.numpy as jnp
from jax import lax
from jax.experimental import pallas as pl
from jax.experimental.pallas import tpu as pltpu
from jax.sharding import PartitionSpec as P

BLOCK = 128
NEAR = 4
BF16 = jnp.bfloat16
F32 = jnp.float32
VMEM_SPEC = pl.BlockSpec(memory_space=pltpu.VMEM)
SMEM_SPEC = pl.BlockSpec(memory_space=pltpu.SMEM)


def near_groups():
    size = lax.axis_size("col")
    return [[z * NEAR + x for x in range(NEAR)] for z in range(size // NEAR)]


def far_groups():
    size = lax.axis_size("col")
    return [[z * NEAR + x for z in range(size // NEAR)] for x in range(NEAR)]


def swap_near(pieces):
    return lax.all_to_all(pieces, "col", 0, 0, axis_index_groups=near_groups(), tiled=True)


def far_size():
    return lax.axis_size("col") // NEAR


def gather_near(value):
    return lax.all_gather(value, "col", axis_index_groups=near_groups(), axis=0)


def copies_of(value, size):
    return jnp.broadcast_to(value.astype(BF16)[None], (size,) + value.shape)


def send_far(copies):
    groups = far_groups()
    return lax.all_to_all(copies, "col", 0, 0, axis_index_groups=groups, tiled=True)


def send_row(copies):
    return lax.all_to_all(copies, "row", 0, 0, tiled=True)


def update_table(blocks, far_at, held):
    targets = far_at * NEAR * held + jnp.arange(NEAR * held, dtype=jnp.int32)
    hits = (blocks[:, None, :] == targets[None, :, None]).astype(jnp.int32)
    return jnp.sum(hits * jnp.arange(1, blocks.shape[1] + 1, dtype=jnp.int32), axis=-1) - 1


def send_col(copies):
    return lax.all_to_all(copies, "col", 0, 0, tiled=True)


def level_mask(sizes, count, start):
    index = start + jnp.arange(count, dtype=jnp.int32)
    return (index[None, :] < sizes[:, None]).astype(F32)[:, None, :]


def dot(a, b, dims):
    return lax.dot_general(a, b, (dims, ((), ())), preferred_element_type=F32)


def call(kernel, out_shape, scalars, arrays, fetched=(), **static):
    specs = [SMEM_SPEC] * len(scalars) + [VMEM_SPEC] * len(arrays)
    specs += [pl.BlockSpec(memory_space=pl.ANY)] * len(fetched)
    scratch = []
    for array in fetched:
        scratch += [pltpu.VMEM(array.shape, array.dtype), pltpu.SemaphoreType.DMA((array.shape[0],))]
    limit = None if fetched else 16 << 20
    return pl.pallas_call(
        functools.partial(kernel, **static),
        out_shape=out_shape,
        in_specs=specs,
        out_specs=jax.tree.map(lambda _: VMEM_SPEC, out_shape),
        scratch_shapes=scratch,
        compiler_params=pltpu.CompilerParams(vmem_limit_bytes=limit),
    )(*scalars, *arrays, *fetched)


def fetch(array, held, semaphores):
    pieces = [
        pltpu.make_async_copy(array.at[x], held.at[x], semaphores.at[x])
        for x in range(array.shape[0])
    ]
    for piece in pieces:
        piece.start()
    return pieces


def pack_kernel(others, inverse, out, held, semaphores):
    rows, n = inverse.shape
    first = pltpu.make_async_copy(inverse, out.at[pl.ds(0, rows)], semaphores.at[0])
    first.start()
    rhs = others.shape[0]
    blocks = others.shape[1] // n
    for k in range(blocks):
        value = others[:, k * n : (k + 1) * n]
        high = value.astype(BF16)
        held[k * rhs : (k + 1) * rhs] = high
        low = (value - high.astype(F32)).astype(BF16)
        held[(blocks + k) * rhs : (blocks + k + 1) * rhs] = low
    second = pltpu.make_async_copy(held, out.at[pl.ds(rows, held.shape[0])], semaphores.at[1])
    second.start()
    first.wait()
    second.wait()


def pack(others, inverse):
    rows, n = inverse.shape
    more = 2 * others.shape[0] * others.shape[1] // n
    anywhere = pl.BlockSpec(memory_space=pl.ANY)
    return pl.pallas_call(
        pack_kernel,
        out_shape=shape_of(rows + more, n),
        in_specs=[VMEM_SPEC, anywhere],
        out_specs=anywhere,
        scratch_shapes=[pltpu.VMEM((more, n), BF16), pltpu.SemaphoreType.DMA((2,))],
    )(others, inverse)


def arrived(parts, f):
    terms = [parts[i, f].astype(F32) for i in range(parts.shape[0])]
    while len(terms) > 1:
        terms = [terms[i] + terms[i + 1] for i in range(0, len(terms), 2)]
    return terms[0]


def write_copies(out, f, value):
    value = value.astype(BF16)
    for i in range(out.shape[0]):
        out[i, f] = value


def shape_of(*dims, dtype=BF16):
    return jax.ShapeDtypeStruct(dims, dtype)


def total_kernel(parts, out):
    terms = [parts[i].astype(F32) for i in range(parts.shape[0])]
    while len(terms) > 1:
        terms = [terms[i] + terms[i + 1] for i in range(0, len(terms), 2)]
    value = terms[0].astype(BF16)
    for i in range(out.shape[0]):
        out[i] = value


def relay_pieces(parts):
    return call(total_kernel, shape_of(*parts.shape), [], [parts])


def first_update_kernel(near, parts, mask, pivots, coupling, out, scaled):
    fronts = coupling.shape[0]
    pieces = parts.shape[0] // fronts
    share = pieces // NEAR
    for f in range(fronts):
        solved = [parts[f * pieces + g].astype(F32) for g in range(pieces)]
        operand = (jnp.concatenate(solved, axis=0) * mask[f]).astype(BF16)
        write_copies(out, f, dot(operand, coupling[f], ((1,), (1,))))
        first = f * pieces + near[0] * share
        solved = [parts[first + g].astype(F32) for g in range(share)]
        scaled[f] = jnp.concatenate(solved, axis=0) * mask[f] * pivots[f]


def first_update(near, parts, mask, pivots, coupling):
    fronts, count, solved = coupling.shape
    rhs = parts.shape[0] * parts.shape[1] // fronts
    out = (
        shape_of(lax.axis_size("row"), fronts, rhs, count),
        shape_of(fronts, rhs // NEAR, solved, dtype=F32),
    )
    return call(first_update_kernel, out, [near], [parts, mask, pivots[:, None, :], coupling])


def last_kernel(got, inverse, out):
    count = inverse.shape[1]
    for f in range(inverse.shape[0]):
        pieces = [got[x, :, f * count : (f + 1) * count].astype(F32) for x in range(NEAR)]
        operand = jnp.concatenate(pieces, axis=0).astype(BF16)
        write_copies(out, f, dot(operand, inverse[f], ((1,), (0,))))


def last_product(got, inverse):
    fronts, _, n = inverse.shape
    out = shape_of(lax.axis_size("row"), fronts, NEAR * got.shape[1], n)
    return call(last_kernel, out, [], [got, inverse])


def scatter_kernel(parts, out):
    width = out.shape[2]
    for f in range(parts.shape[1]):
        value = arrived(parts, f)
        for x in range(NEAR):
            share = value[x * width : (x + 1) * width].astype(BF16)
            for z in range(out.shape[0] // NEAR):
                out[z * NEAR + x, f] = share


def relay_scattered(parts):
    _, fronts, rhs, count = parts.shape
    out = shape_of(lax.axis_size("col"), fronts, rhs // NEAR, count)
    return call(scatter_kernel, out, [], [parts])


def update_kernel(parts, mask, pivots, coupling, out, scaled):
    for f in range(parts.shape[1]):
        solved = arrived(parts, f) * mask[f]
        scaled[f] = solved * pivots[f]
        operand = solved.astype(BF16)
        update = [dot(operand, coupling[x, f], ((1,), (1,))) for x in range(NEAR)]
        write_copies(out, f, jnp.concatenate(update, axis=-1))


def update_of(parts, mask, pivots, coupling):
    _, fronts, width, count = parts.shape
    rows = lax.axis_size("row")
    out = (
        shape_of(rows, fronts, width, NEAR * coupling.shape[2]),
        shape_of(fronts, width, count, dtype=F32),
    )
    return call(update_kernel, out, [], [parts, mask, pivots[:, None, :], coupling])


def relay_kernel(parts, out):
    for f in range(parts.shape[1]):
        write_copies(out, f, arrived(parts, f))


def relay(parts):
    return call(relay_kernel, shape_of(far_size(), *parts.shape[1:]), [], [parts])


def solved_kernel(parts, mask, out, solved):
    for f in range(parts.shape[1]):
        value = arrived(parts, f) * mask[f]
        solved[f] = value
        write_copies(out, f, value)


def relay_solved(parts, mask):
    shape = parts.shape[1:]
    out = (shape_of(far_size(), *shape), shape_of(*shape, dtype=F32))
    return call(solved_kernel, out, [], [parts, mask])


def source_tile(source, x, start):
    blocks, n = source.shape[1] // 2, source.shape[3]
    k, lanes = start // n, slice(start % n, start % n + BLOCK)
    high = source[x, k, :, lanes].astype(F32)
    return high + source[x, blocks + k, :, lanes].astype(F32)


def place_kernel(table, whole, source, mask, inverse_at, out, inverse, semaphores, *, base):
    copies = fetch(inverse_at, inverse, semaphores)
    n = inverse.shape[2]
    held = n // BLOCK
    count = out.shape[3]
    spread = whole.shape[3] // BLOCK
    for p in range(out.shape[1]):
        total = None
        for x in range(NEAR):
            tiles = []
            for b in range(held):
                start = base + p * n + b * BLOCK
                tile = source_tile(source, x, start)
                for c in (2 * p, 2 * p + 1):
                    at = table[c, x * held + b]
                    found = jnp.where(at >= 0, 1.0, 0.0).astype(F32)
                    at = jnp.maximum(at, 0)
                    if spread == 1:
                        placed = whole[at, c]
                    else:
                        lane = pl.multiple_of((at % spread) * BLOCK, BLOCK)
                        placed = whole[at // spread, c, :, pl.ds(lane, BLOCK)]
                    tile = tile - placed.astype(F32) * found
                tiles.append(tile)
            operand = jnp.concatenate(tiles, axis=-1) * mask[p, :, x * n : (x + 1) * n]
            if p == 0:
                copies[x].wait()
            rows = inverse[x, p * count : (p + 1) * count]
            part = dot(operand.astype(BF16), rows, ((1,), (1,)))
            total = part if total is None else total + part
        write_copies(out, p, total)


def place_and_solve(table, whole, source, mask, inverse, parents, count, base):
    out = shape_of(far_size(), parents, whole.shape[2], count)
    return call(place_kernel, out, [table], [whole, source, mask], [inverse], base=base)


def root_kernel(parts, pivots, inverse_at, out, inverse, semaphores):
    copies = fetch(inverse_at, inverse, semaphores)
    operand = (arrived(parts, 0) * pivots[...]).astype(BF16)
    pieces = []
    for x in range(NEAR):
        copies[x].wait()
        pieces.append(dot(operand, inverse[x], ((1,), (0,))))
    write_copies(out, 0, jnp.concatenate(pieces, axis=-1))


def root_back(parts, pivots, inverse):
    out = shape_of(lax.axis_size("row"), 1, parts.shape[2], NEAR * inverse.shape[2])
    return call(root_kernel, out, [], [parts, pivots[None, :]], [inverse])


def back_kernel(parts, scaled, mask, inverse, out):
    count = parts.shape[3]
    for p in range(parts.shape[1]):
        operand = ((scaled[p] - arrived(parts, p)) * mask[p]).astype(BF16)
        pieces = [
            dot(operand, inverse[x, p * count : (p + 1) * count], ((1,), (0,)))
            for x in range(NEAR)
        ]
        write_copies(out, p, jnp.concatenate(pieces, axis=-1))


def back(parts, scaled, mask, inverse):
    _, fronts, width, _ = parts.shape
    out = shape_of(lax.axis_size("row"), fronts, width, NEAR * inverse.shape[2])
    return call(back_kernel, out, [], [parts, scaled, mask, inverse])


def pick_kernel(far, blocks, whole, coupling, out, copies=None):
    held = whole.shape[3] // BLOCK
    for c in range(blocks.shape[0]):
        total = None
        for x in range(NEAR):
            block = blocks[c, far[0] * NEAR + x]
            lane = pl.multiple_of((block % held) * BLOCK, BLOCK)
            tile = whole[block // held, c // 2, :, pl.ds(lane, BLOCK)]
            if copies is not None and c == 0:
                copies[x].wait()
            part = dot(tile, coupling[x, c], ((1,), (0,)))
            total = part if total is None else total + part
        write_copies(out, c, total)


def pick_and_carry(far, blocks, whole, coupling):
    _, children, _, count = coupling.shape
    out = shape_of(far_size(), children, whole.shape[2], count)
    return call(pick_kernel, out, [far, blocks], [whole, coupling])


def pick_fetched_kernel(far, blocks, whole, coupling_at, out, coupling, semaphores):
    copies = fetch(coupling_at, coupling, semaphores)
    pick_kernel(far, blocks, whole, coupling, out, copies)


def pick_fetched(far, blocks, whole, coupling):
    _, children, _, count = coupling.shape
    out = shape_of(far_size(), children, whole.shape[2], count)
    return call(pick_fetched_kernel, out, [far, blocks], [whole], [coupling])


def halves(value):
    high = value.astype(BF16)
    return high, (value - high.astype(F32)).astype(BF16)


def local(
    inverse_top,
    inverse_mid,
    inverse_low,
    coupling_mid,
    coupling_low,
    source_top,
    source_mid,
    source_low,
    pivots_top,
    pivots_mid,
    pivots_low,
    sizes_mid,
    sizes_low,
    blocks_mid,
    blocks_low,
):
    row_at = lax.axis_index("row")
    col_at = lax.axis_index("col")
    far_at = col_at // NEAR
    rhs = source_top.shape[1]
    width = rhs // NEAR
    n0, n1, n2 = source_top.shape[0], source_mid.shape[1], source_low.shape[1]
    k1, k2 = inverse_mid.shape[1], inverse_low.shape[1]
    top = jnp.full((1,), inverse_top.shape[0] * lax.axis_size("row"), jnp.int32)

    far, near = far_at.reshape(1), (col_at % NEAR).reshape(1)
    table_low = update_table(blocks_low, far_at, n1 // BLOCK)
    table_mid = update_table(blocks_mid, far_at, n0 // BLOCK)
    row_mask_mid = level_mask(sizes_mid, k1, row_at * k1)
    row_mask_low = level_mask(sizes_low, k2, row_at * k2)
    col_mask_low = level_mask(sizes_low, n2, col_at * n2)
    wide_mask_mid = level_mask(sizes_mid, NEAR * n1, far_at * NEAR * n1)
    wide_mask_top = level_mask(top, NEAR * n0, far_at * NEAR * n0)

    source = jnp.swapaxes(source_low, 1, 2) * col_mask_low
    partial = jnp.einsum(
        "fij,fcj->fci", inverse_low, source.astype(BF16), preferred_element_type=F32
    )
    message = partial.astype(BF16).reshape(lax.axis_size("col"), -1, k2)

    coupling_mid_near = gather_near(coupling_mid)
    inverse_mid, source_mid, source_top, message = lax.optimization_barrier(
        (inverse_mid, source_mid, source_top, message)
    )
    others = jnp.concatenate([source_mid[0].T, source_mid[1].T, source_top.T], axis=-1)
    others = jnp.pad(others, ((0, 0), (0, -others.shape[1] % n1)))
    packed = pack(others, inverse_mid.reshape(-1, n1))
    packed, inverse_top, coupling_low_late = lax.optimization_barrier(
        (packed, inverse_top, coupling_low)
    )
    packed_near = gather_near(packed)
    inverse_top_near = gather_near(inverse_top)
    coupling_low_near = gather_near(coupling_low_late)

    parts = send_col(relay_pieces(send_col(message)))
    message, scaled_low = first_update(near, parts, row_mask_low, pivots_low, coupling_low)
    whole = send_col(relay_scattered(send_row(message)))

    others = packed_near[:, 2 * k1 :].reshape(NEAR, -1, rhs, n1)
    others = lax.dynamic_slice_in_dim(others, (col_at % NEAR) * width, width, 2)
    message = place_and_solve(table_low, whole, others, wide_mask_mid, packed_near, 2, k1, 0)
    parts = send_far(message)

    message, scaled_mid = update_of(parts, row_mask_mid, pivots_mid, coupling_mid_near)
    whole = send_far(relay(send_row(message)))
    k0 = inverse_top.shape[0]
    parts = send_far(
        place_and_solve(table_mid, whole, others, wide_mask_top, inverse_top_near, 1, k0, 2 * n1)
    )

    message, solution_top = relay_solved(
        send_row(root_back(parts, pivots_top, inverse_top_near)), wide_mask_top
    )
    message = pick_and_carry(far, blocks_mid, send_far(message), coupling_mid_near)
    parts = send_far(message)
    message, solution_mid = relay_solved(
        send_row(back(parts, scaled_mid, row_mask_mid, packed_near)), wide_mask_mid
    )
    parts = send_far(pick_fetched(far, blocks_low, send_far(message), coupling_low_near))
    residual = (scaled_low - jnp.sum(parts.astype(F32), axis=0)) * row_mask_low

    upper = jnp.concatenate(
        [
            solution_top[0].reshape(width, NEAR, n0),
            solution_mid[0].reshape(width, NEAR, n1),
            solution_mid[1].reshape(width, NEAR, n1),
        ],
        axis=-1,
    )
    upper = jnp.swapaxes(jnp.concatenate(halves(upper), axis=-1), 0, 1)
    flat = jnp.swapaxes(residual, 0, 1).reshape(width, -1).astype(BF16)
    size = flat.shape[1]
    message = jnp.concatenate([copies_of(flat, NEAR), upper], axis=-1)
    got = swap_near(message)
    parts = send_row(last_product(got, inverse_low))
    upper = got[:, :, size:].astype(F32).reshape(rhs, -1)
    upper = upper[:, : upper.shape[1] // 2] + upper[:, upper.shape[1] // 2 :]
    solution_low = jnp.sum(parts.astype(F32), axis=0) * col_mask_low
    return (
        upper[:, :n0].T,
        jnp.stack([upper[:, n0 : n0 + n1].T, upper[:, n0 + n1 :].T]),
        jnp.swapaxes(solution_low, 1, 2),
    )


def solution(mesh):
    placed = (
        P("row", "col"),
        P(None, "row", "col"),
        P(None, "row", "col"),
        P(None, "col", "row"),
        P(None, "col", "row"),
        P("col", None),
        P(None, "col", None),
        P(None, "col", None),
        P("row"),
        P(None, "row"),
        P(None, "row"),
        P(),
        P(),
        P(),
        P(),
    )
    return jax.shard_map(
        local,
        mesh=mesh,
        in_specs=placed,
        out_specs=(P("col", None), P(None, "col", None), P(None, "col", None)),
        check_vma=False,
    )
```

```python
import functools

import jax
import jax.numpy as jnp
from jax import lax
from jax.experimental import pallas as pl
from jax.experimental.pallas import tpu as pltpu
from jax.sharding import PartitionSpec as P

BLOCK = 128
NEAR = 4
BF16 = jnp.bfloat16
F32 = jnp.float32
VMEM_SPEC = pl.BlockSpec(memory_space=pltpu.VMEM)
SMEM_SPEC = pl.BlockSpec(memory_space=pltpu.SMEM)


def near_groups():
    size = lax.axis_size("col")
    return [[z * NEAR + x for x in range(NEAR)] for z in range(size // NEAR)]


def far_groups():
    size = lax.axis_size("col")
    return [[z * NEAR + x for z in range(size // NEAR)] for x in range(NEAR)]


def swap_near(pieces):
    return lax.all_to_all(pieces, "col", 0, 0, axis_index_groups=near_groups(), tiled=True)


def far_size():
    return lax.axis_size("col") // NEAR


def gather_near(value):
    return lax.all_gather(value, "col", axis_index_groups=near_groups(), axis=0)


def copies_of(value, size):
    return jnp.broadcast_to(value.astype(BF16)[None], (size,) + value.shape)


def send_far(copies):
    groups = far_groups()
    return lax.all_to_all(copies, "col", 0, 0, axis_index_groups=groups, tiled=True)


def send_row(copies):
    return lax.all_to_all(copies, "row", 0, 0, tiled=True)


def update_table(blocks, far_at, held):
    targets = far_at * NEAR * held + jnp.arange(NEAR * held, dtype=jnp.int32)
    hits = (blocks[:, None, :] == targets[None, :, None]).astype(jnp.int32)
    return jnp.sum(hits * jnp.arange(1, blocks.shape[1] + 1, dtype=jnp.int32), axis=-1) - 1


def send_col(copies):
    return lax.all_to_all(copies, "col", 0, 0, tiled=True)


def level_mask(sizes, count, start):
    index = start + jnp.arange(count, dtype=jnp.int32)
    return (index[None, :] < sizes[:, None]).astype(F32)[:, None, :]


def dot(a, b, dims):
    return lax.dot_general(a, b, (dims, ((), ())), preferred_element_type=F32)


def call(kernel, out_shape, scalars, arrays, **static):
    return pl.pallas_call(
        functools.partial(kernel, **static),
        out_shape=out_shape,
        in_specs=[SMEM_SPEC] * len(scalars) + [VMEM_SPEC] * len(arrays),
        out_specs=jax.tree.map(lambda _: VMEM_SPEC, out_shape),
        compiler_params=pltpu.CompilerParams(vmem_limit_bytes=16 << 20),
    )(*scalars, *arrays)


LANES = 128


def tall(operand):
    missing = jnp.zeros((LANES - operand.shape[0], operand.shape[1]), F32)
    return jnp.concatenate([operand, missing], axis=0).astype(BF16)


def times_tall(matrix, operand):
    return dot(matrix, operand, ((1,), (1,)))


def arrived(parts, f):
    terms = [parts[i, f].astype(F32) for i in range(parts.shape[0])]
    while len(terms) > 1:
        terms = [terms[i] + terms[i + 1] for i in range(0, len(terms), 2)]
    return terms[0]


def write_copies(out, f, value):
    value = value.astype(BF16)
    for i in range(out.shape[0]):
        out[i, f] = value


def shape_of(*dims, dtype=BF16):
    return jax.ShapeDtypeStruct(dims, dtype)


def total_kernel(parts, out):
    terms = [parts[i].astype(F32) for i in range(parts.shape[0])]
    while len(terms) > 1:
        terms = [terms[i] + terms[i + 1] for i in range(0, len(terms), 2)]
    value = terms[0].astype(BF16)
    for i in range(out.shape[0]):
        out[i] = value


def relay_pieces(parts):
    return call(total_kernel, shape_of(*parts.shape), [], [parts])


def first_update_kernel(near, parts, mask, pivots, coupling, out, scaled):
    fronts = coupling.shape[0]
    pieces = parts.shape[0] // fronts
    share = pieces // NEAR
    for f in range(fronts):
        solved = [parts[f * pieces + g].astype(F32) for g in range(pieces)]
        operand = tall(jnp.concatenate(solved, axis=0) * mask[f])
        write_copies(out, f, times_tall(coupling[f], operand).T[: out.shape[2]])
        first = f * pieces + near[0] * share
        solved = [parts[first + g].astype(F32) for g in range(share)]
        scaled[f] = jnp.concatenate(solved, axis=0) * mask[f] * pivots[f]


def first_update(near, parts, mask, pivots, coupling):
    fronts, count, solved = coupling.shape
    rhs = parts.shape[0] * parts.shape[1] // fronts
    out = (
        shape_of(lax.axis_size("row"), fronts, rhs, count),
        shape_of(fronts, rhs // NEAR, solved, dtype=F32),
    )
    return call(first_update_kernel, out, [near], [parts, mask, pivots[:, None, :], coupling])


def last_kernel(got, inverse, out):
    count = inverse.shape[1]
    for f in range(inverse.shape[0]):
        pieces = [got[x, :, f * count : (f + 1) * count].astype(F32) for x in range(NEAR)]
        operand = jnp.concatenate(pieces, axis=0).astype(BF16)
        write_copies(out, f, dot(operand, inverse[f], ((1,), (0,))))


def last_product(got, inverse):
    fronts, _, n = inverse.shape
    out = shape_of(lax.axis_size("row"), fronts, NEAR * got.shape[1], n)
    return call(last_kernel, out, [], [got, inverse])


def scatter_kernel(parts, out):
    width = out.shape[2]
    for f in range(parts.shape[1]):
        value = arrived(parts, f)
        for x in range(NEAR):
            share = value[x * width : (x + 1) * width].astype(BF16)
            for z in range(out.shape[0] // NEAR):
                out[z * NEAR + x, f] = share


def relay_scattered(parts):
    _, fronts, rhs, count = parts.shape
    out = shape_of(lax.axis_size("col"), fronts, rhs // NEAR, count)
    return call(scatter_kernel, out, [], [parts])


def update_kernel(parts, mask, pivots, coupling, out, scaled):
    for f in range(parts.shape[1]):
        solved = arrived(parts, f) * mask[f]
        scaled[f] = solved * pivots[f]
        operand = tall(solved)
        update = [times_tall(coupling[x, f], operand).T[: out.shape[2]] for x in range(NEAR)]
        write_copies(out, f, jnp.concatenate(update, axis=-1))


def update_of(parts, mask, pivots, coupling):
    _, fronts, width, count = parts.shape
    rows = lax.axis_size("row")
    out = (
        shape_of(rows, fronts, width, NEAR * coupling.shape[2]),
        shape_of(fronts, width, count, dtype=F32),
    )
    return call(update_kernel, out, [], [parts, mask, pivots[:, None, :], coupling])


def relay_kernel(parts, out):
    for f in range(parts.shape[1]):
        write_copies(out, f, arrived(parts, f))


def relay(parts):
    return call(relay_kernel, shape_of(far_size(), *parts.shape[1:]), [], [parts])


def solved_kernel(parts, mask, out, solved):
    for f in range(parts.shape[1]):
        value = arrived(parts, f) * mask[f]
        solved[f] = value
        write_copies(out, f, value)


def relay_solved(parts, mask):
    shape = parts.shape[1:]
    out = (shape_of(far_size(), *shape), shape_of(*shape, dtype=F32))
    return call(solved_kernel, out, [], [parts, mask])


def place_kernel(table, whole, source, mask, inverse, out, *, base):
    n = inverse.shape[2]
    held = n // BLOCK
    count = out.shape[3]
    spread = whole.shape[3] // BLOCK
    for p in range(out.shape[1]):
        total = None
        for x in range(NEAR):
            tiles = []
            for b in range(held):
                start = base + p * n + b * BLOCK
                tile = source[x, :, start : start + BLOCK]
                for c in (2 * p, 2 * p + 1):
                    at = table[c, x * held + b]
                    found = jnp.where(at >= 0, 1.0, 0.0).astype(F32)
                    at = jnp.maximum(at, 0)
                    if spread == 1:
                        placed = whole[at, c]
                    else:
                        lane = pl.multiple_of((at % spread) * BLOCK, BLOCK)
                        placed = whole[at // spread, c, :, pl.ds(lane, BLOCK)]
                    tile = tile - placed.astype(F32) * found
                tiles.append(tile)
            operand = jnp.concatenate(tiles, axis=-1) * mask[p, :, x * n : (x + 1) * n]
            rows = inverse[x, p * count : (p + 1) * count]
            part = times_tall(rows, tall(operand))
            total = part if total is None else total + part
        write_copies(out, p, total.T[: out.shape[2]])


def place_and_solve(table, whole, source, mask, inverse, parents, count, base):
    out = shape_of(far_size(), parents, whole.shape[2], count)
    return call(place_kernel, out, [table], [whole, source, mask, inverse], base=base)


def root_kernel(parts, pivots, inverse, out):
    operand = (arrived(parts, 0) * pivots[...]).astype(BF16)
    pieces = [dot(operand, inverse[x], ((1,), (0,))) for x in range(NEAR)]
    write_copies(out, 0, jnp.concatenate(pieces, axis=-1))


def root_back(parts, pivots, inverse):
    out = shape_of(lax.axis_size("row"), 1, parts.shape[2], NEAR * inverse.shape[2])
    return call(root_kernel, out, [], [parts, pivots[None, :], inverse])


def back_kernel(parts, scaled, mask, inverse, out):
    count = parts.shape[3]
    for p in range(parts.shape[1]):
        operand = ((scaled[p] - arrived(parts, p)) * mask[p]).astype(BF16)
        pieces = [
            dot(operand, inverse[x, p * count : (p + 1) * count], ((1,), (0,)))
            for x in range(NEAR)
        ]
        write_copies(out, p, jnp.concatenate(pieces, axis=-1))


def back(parts, scaled, mask, inverse):
    _, fronts, width, _ = parts.shape
    out = shape_of(lax.axis_size("row"), fronts, width, NEAR * inverse.shape[2])
    return call(back_kernel, out, [], [parts, scaled, mask, inverse])


def pick_kernel(far, blocks, whole, coupling, out):
    held = whole.shape[3] // BLOCK
    for c in range(blocks.shape[0]):
        total = None
        for x in range(NEAR):
            block = blocks[c, far[0] * NEAR + x]
            lane = pl.multiple_of((block % held) * BLOCK, BLOCK)
            tile = whole[block // held, c // 2, :, pl.ds(lane, BLOCK)]
            part = dot(tile, coupling[x, c], ((1,), (0,)))
            total = part if total is None else total + part
        write_copies(out, c, total)


def pick_and_carry(far, blocks, whole, coupling):
    _, children, _, count = coupling.shape
    out = shape_of(far_size(), children, whole.shape[2], count)
    return call(pick_kernel, out, [far, blocks], [whole, coupling])


def halves(value):
    high = value.astype(BF16)
    return high, (value - high.astype(F32)).astype(BF16)


def local(
    inverse_top,
    inverse_mid,
    inverse_low,
    coupling_mid,
    coupling_low,
    source_top,
    source_mid,
    source_low,
    pivots_top,
    pivots_mid,
    pivots_low,
    sizes_mid,
    sizes_low,
    blocks_mid,
    blocks_low,
):
    row_at = lax.axis_index("row")
    col_at = lax.axis_index("col")
    far_at = col_at // NEAR
    rhs = source_top.shape[1]
    width = rhs // NEAR
    n0, n1, n2 = source_top.shape[0], source_mid.shape[1], source_low.shape[1]
    k1, k2 = inverse_mid.shape[1], inverse_low.shape[1]
    top = jnp.full((1,), inverse_top.shape[0] * lax.axis_size("row"), jnp.int32)

    far, near = far_at.reshape(1), (col_at % NEAR).reshape(1)
    table_low = update_table(blocks_low, far_at, n1 // BLOCK)
    table_mid = update_table(blocks_mid, far_at, n0 // BLOCK)
    row_mask_mid = level_mask(sizes_mid, k1, row_at * k1)
    row_mask_low = level_mask(sizes_low, k2, row_at * k2)
    col_mask_low = level_mask(sizes_low, n2, col_at * n2)
    wide_mask_mid = level_mask(sizes_mid, NEAR * n1, far_at * NEAR * n1)
    wide_mask_top = level_mask(top, NEAR * n0, far_at * NEAR * n0)

    source = jnp.swapaxes(source_low, 1, 2) * col_mask_low
    partial = jnp.einsum(
        "fij,fcj->fci", inverse_low, source.astype(BF16), preferred_element_type=F32
    )
    message = partial.astype(BF16).reshape(lax.axis_size("col"), -1, k2)

    coupling_mid_near = gather_near(coupling_mid)
    inverse_mid, source_mid, source_top, message = lax.optimization_barrier(
        (inverse_mid, source_mid, source_top, message)
    )
    others = jnp.concatenate([source_mid[0].T, source_mid[1].T, source_top.T], axis=-1)
    halved = jnp.concatenate(halves(others), axis=-1).reshape(-1, n1)
    packed = jnp.concatenate([inverse_mid.reshape(-1, n1), halved], axis=0)
    packed, inverse_top, coupling_low_late = lax.optimization_barrier(
        (packed, inverse_top, coupling_low)
    )
    packed_near = gather_near(packed)
    inverse_top_near = gather_near(inverse_top)
    coupling_low_near = gather_near(coupling_low_late)

    parts = send_col(relay_pieces(send_col(message)))
    message, scaled_low = first_update(near, parts, row_mask_low, pivots_low, coupling_low)
    whole = send_col(relay_scattered(send_row(message)))

    halved = packed_near[:, 2 * k1 :].reshape(NEAR, rhs, -1)
    halved = lax.dynamic_slice_in_dim(halved, (col_at % NEAR) * width, width, 1).astype(F32)
    size = halved.shape[2] // 2
    others = halved[:, :, :size] + halved[:, :, size:]
    message = place_and_solve(table_low, whole, others, wide_mask_mid, packed_near, 2, k1, 0)
    parts = send_far(message)

    message, scaled_mid = update_of(parts, row_mask_mid, pivots_mid, coupling_mid_near)
    whole = send_far(relay(send_row(message)))
    k0 = inverse_top.shape[0]
    parts = send_far(
        place_and_solve(table_mid, whole, others, wide_mask_top, inverse_top_near, 1, k0, 2 * n1)
    )

    message, solution_top = relay_solved(
        send_row(root_back(parts, pivots_top, inverse_top_near)), wide_mask_top
    )
    message = pick_and_carry(far, blocks_mid, send_far(message), coupling_mid_near)
    parts = send_far(message)
    message, solution_mid = relay_solved(
        send_row(back(parts, scaled_mid, row_mask_mid, packed_near)), wide_mask_mid
    )
    parts = send_far(pick_and_carry(far, blocks_low, send_far(message), coupling_low_near))
    residual = (scaled_low - jnp.sum(parts.astype(F32), axis=0)) * row_mask_low

    upper = jnp.concatenate(
        [
            solution_top[0].reshape(width, NEAR, n0),
            solution_mid[0].reshape(width, NEAR, n1),
            solution_mid[1].reshape(width, NEAR, n1),
        ],
        axis=-1,
    )
    upper = jnp.swapaxes(jnp.concatenate(halves(upper), axis=-1), 0, 1)
    flat = jnp.swapaxes(residual, 0, 1).reshape(width, -1).astype(BF16)
    size = flat.shape[1]
    message = jnp.concatenate([copies_of(flat, NEAR), upper], axis=-1)
    got = swap_near(message)
    parts = send_row(last_product(got, inverse_low))
    upper = got[:, :, size:].astype(F32).reshape(rhs, -1)
    upper = upper[:, : upper.shape[1] // 2] + upper[:, upper.shape[1] // 2 :]
    solution_low = jnp.sum(parts.astype(F32), axis=0) * col_mask_low
    return (
        upper[:, :n0].T,
        jnp.stack([upper[:, n0 : n0 + n1].T, upper[:, n0 + n1 :].T]),
        jnp.swapaxes(solution_low, 1, 2),
    )


def solution(mesh):
    placed = (
        P("row", "col"),
        P(None, "row", "col"),
        P(None, "row", "col"),
        P(None, "col", "row"),
        P(None, "col", "row"),
        P("col", None),
        P(None, "col", None),
        P(None, "col", None),
        P("row"),
        P(None, "row"),
        P(None, "row"),
        P(),
        P(),
        P(),
        P(),
    )
    return jax.shard_map(
        local,
        mesh=mesh,
        in_specs=placed,
        out_specs=(P("col", None), P(None, "col", None), P(None, "col", None)),
        check_vma=False,
    )
```

```python
import functools

import jax
import jax.numpy as jnp
from jax import lax
from jax.experimental import pallas as pl
from jax.experimental.pallas import tpu as pltpu
from jax.sharding import PartitionSpec as P

BLOCK = 128
NEAR = 4
BF16 = jnp.bfloat16
F32 = jnp.float32
VMEM_SPEC = pl.BlockSpec(memory_space=pltpu.VMEM)
SMEM_SPEC = pl.BlockSpec(memory_space=pltpu.SMEM)


def near_groups():
    size = lax.axis_size("col")
    return [[z * NEAR + x for x in range(NEAR)] for z in range(size // NEAR)]


def far_groups():
    size = lax.axis_size("col")
    return [[z * NEAR + x for z in range(size // NEAR)] for x in range(NEAR)]


def swap_near(pieces):
    return lax.all_to_all(pieces, "col", 0, 0, axis_index_groups=near_groups(), tiled=True)


def far_size():
    return lax.axis_size("col") // NEAR


def gather_near(value):
    return lax.all_gather(value, "col", axis_index_groups=near_groups(), axis=0)


def settled(array, message):
    zero = lax.slice(message, (0,) * message.ndim, (1,) * message.ndim).reshape(()) * 0
    return array + zero.astype(array.dtype)


def copies_of(value, size):
    return jnp.broadcast_to(value.astype(BF16)[None], (size,) + value.shape)


def send_far(copies):
    groups = far_groups()
    return lax.all_to_all(copies, "col", 0, 0, axis_index_groups=groups, tiled=True)


def send_row(copies):
    return lax.all_to_all(copies, "row", 0, 0, tiled=True)


def update_table(blocks, far_at, held):
    targets = far_at * NEAR * held + jnp.arange(NEAR * held, dtype=jnp.int32)
    hits = (blocks[:, None, :] == targets[None, :, None]).astype(jnp.int32)
    return jnp.sum(hits * jnp.arange(1, blocks.shape[1] + 1, dtype=jnp.int32), axis=-1) - 1


def send_col(copies):
    return lax.all_to_all(copies, "col", 0, 0, tiled=True)


def level_mask(sizes, count, start):
    index = start + jnp.arange(count, dtype=jnp.int32)
    return (index[None, :] < sizes[:, None]).astype(F32)[:, None, :]


def dot(a, b, dims):
    return lax.dot_general(a, b, (dims, ((), ())), preferred_element_type=F32)


def call(kernel, out_shape, scalars, arrays, **static):
    return pl.pallas_call(
        functools.partial(kernel, **static),
        out_shape=out_shape,
        in_specs=[SMEM_SPEC] * len(scalars) + [VMEM_SPEC] * len(arrays),
        out_specs=jax.tree.map(lambda _: VMEM_SPEC, out_shape),
        compiler_params=pltpu.CompilerParams(vmem_limit_bytes=16 << 20),
    )(*scalars, *arrays)


LANES = 128


def tall(operand):
    missing = jnp.zeros((LANES - operand.shape[0], operand.shape[1]), F32)
    return jnp.concatenate([operand, missing], axis=0).astype(BF16)


def times_tall(matrix, operand):
    return dot(matrix, operand, ((1,), (1,)))


def arrived(parts, f):
    terms = [parts[i, f].astype(F32) for i in range(parts.shape[0])]
    while len(terms) > 1:
        terms = [terms[i] + terms[i + 1] for i in range(0, len(terms), 2)]
    return terms[0]


def write_copies(out, f, value):
    value = value.astype(BF16)
    for i in range(out.shape[0]):
        out[i, f] = value


def shape_of(*dims, dtype=BF16):
    return jax.ShapeDtypeStruct(dims, dtype)


def total_kernel(parts, out):
    terms = [parts[i].astype(F32) for i in range(parts.shape[0])]
    while len(terms) > 1:
        terms = [terms[i] + terms[i + 1] for i in range(0, len(terms), 2)]
    value = terms[0].astype(BF16)
    for i in range(out.shape[0]):
        out[i] = value


def relay_pieces(parts):
    return call(total_kernel, shape_of(*parts.shape), [], [parts])


def first_update_kernel(near, parts, mask, pivots, coupling, out, scaled):
    fronts = coupling.shape[0]
    pieces = parts.shape[0] // fronts
    share = pieces // NEAR
    for f in range(fronts):
        solved = [parts[f * pieces + g].astype(F32) for g in range(pieces)]
        operand = tall(jnp.concatenate(solved, axis=0) * mask[f])
        write_copies(out, f, times_tall(coupling[f], operand).T[: out.shape[2]])
        first = f * pieces + near[0] * share
        solved = [parts[first + g].astype(F32) for g in range(share)]
        scaled[f] = jnp.concatenate(solved, axis=0) * mask[f] * pivots[f]


def first_update(near, parts, mask, pivots, coupling):
    fronts, count, solved = coupling.shape
    rhs = parts.shape[0] * parts.shape[1] // fronts
    out = (
        shape_of(lax.axis_size("row"), fronts, rhs, count),
        shape_of(fronts, rhs // NEAR, solved, dtype=F32),
    )
    return call(first_update_kernel, out, [near], [parts, mask, pivots[:, None, :], coupling])


def last_kernel(got, inverse, out):
    count = inverse.shape[1]
    for f in range(inverse.shape[0]):
        pieces = [got[x, :, f * count : (f + 1) * count].astype(F32) for x in range(NEAR)]
        operand = jnp.concatenate(pieces, axis=0).astype(BF16)
        write_copies(out, f, dot(operand, inverse[f], ((1,), (0,))))


def last_product(got, inverse):
    fronts, _, n = inverse.shape
    out = shape_of(lax.axis_size("row"), fronts, NEAR * got.shape[1], n)
    return call(last_kernel, out, [], [got, inverse])


def scatter_kernel(parts, out):
    width = out.shape[2]
    for f in range(parts.shape[1]):
        value = arrived(parts, f)
        for x in range(NEAR):
            share = value[x * width : (x + 1) * width].astype(BF16)
            for z in range(out.shape[0] // NEAR):
                out[z * NEAR + x, f] = share


def relay_scattered(parts):
    _, fronts, rhs, count = parts.shape
    out = shape_of(lax.axis_size("col"), fronts, rhs // NEAR, count)
    return call(scatter_kernel, out, [], [parts])


def update_kernel(parts, mask, pivots, coupling, out, scaled):
    for f in range(parts.shape[1]):
        solved = arrived(parts, f) * mask[f]
        scaled[f] = solved * pivots[f]
        operand = tall(solved)
        update = [times_tall(coupling[x, f], operand).T[: out.shape[2]] for x in range(NEAR)]
        write_copies(out, f, jnp.concatenate(update, axis=-1))


def update_of(parts, mask, pivots, coupling):
    _, fronts, width, count = parts.shape
    rows = lax.axis_size("row")
    out = (
        shape_of(rows, fronts, width, NEAR * coupling.shape[2]),
        shape_of(fronts, width, count, dtype=F32),
    )
    return call(update_kernel, out, [], [parts, mask, pivots[:, None, :], coupling])


def relay_kernel(parts, out):
    for f in range(parts.shape[1]):
        write_copies(out, f, arrived(parts, f))


def relay(parts):
    return call(relay_kernel, shape_of(far_size(), *parts.shape[1:]), [], [parts])


def solved_kernel(parts, mask, out, solved):
    for f in range(parts.shape[1]):
        value = arrived(parts, f) * mask[f]
        solved[f] = value
        write_copies(out, f, value)


def relay_solved(parts, mask):
    shape = parts.shape[1:]
    out = (shape_of(far_size(), *shape), shape_of(*shape, dtype=F32))
    return call(solved_kernel, out, [], [parts, mask])


def place_kernel(table, whole, source, mask, inverse, out, *, base):
    n = inverse.shape[2]
    held = n // BLOCK
    count = out.shape[3]
    spread = whole.shape[3] // BLOCK
    for p in range(out.shape[1]):
        total = None
        for x in range(NEAR):
            tiles = []
            for b in range(held):
                start = base + p * n + b * BLOCK
                tile = source[x, :, start : start + BLOCK]
                for c in (2 * p, 2 * p + 1):
                    at = table[c, x * held + b]
                    found = jnp.where(at >= 0, 1.0, 0.0).astype(F32)
                    at = jnp.maximum(at, 0)
                    if spread == 1:
                        placed = whole[at, c]
                    else:
                        lane = pl.multiple_of((at % spread) * BLOCK, BLOCK)
                        placed = whole[at // spread, c, :, pl.ds(lane, BLOCK)]
                    tile = tile - placed.astype(F32) * found
                tiles.append(tile)
            operand = jnp.concatenate(tiles, axis=-1) * mask[p, :, x * n : (x + 1) * n]
            rows = inverse[x, p * count : (p + 1) * count]
            part = times_tall(rows, tall(operand))
            total = part if total is None else total + part
        write_copies(out, p, total.T[: out.shape[2]])


def place_and_solve(table, whole, source, mask, inverse, parents, count, base):
    out = shape_of(far_size(), parents, whole.shape[2], count)
    return call(place_kernel, out, [table], [whole, source, mask, inverse], base=base)


def root_kernel(parts, pivots, inverse, out):
    operand = (arrived(parts, 0) * pivots[...]).astype(BF16)
    pieces = [dot(operand, inverse[x], ((1,), (0,))) for x in range(NEAR)]
    write_copies(out, 0, jnp.concatenate(pieces, axis=-1))


def root_back(parts, pivots, inverse):
    out = shape_of(lax.axis_size("row"), 1, parts.shape[2], NEAR * inverse.shape[2])
    return call(root_kernel, out, [], [parts, pivots[None, :], inverse])


def back_kernel(parts, scaled, mask, inverse, out):
    count = parts.shape[3]
    for p in range(parts.shape[1]):
        operand = ((scaled[p] - arrived(parts, p)) * mask[p]).astype(BF16)
        pieces = [
            dot(operand, inverse[x, p * count : (p + 1) * count], ((1,), (0,)))
            for x in range(NEAR)
        ]
        write_copies(out, p, jnp.concatenate(pieces, axis=-1))


def back(parts, scaled, mask, inverse):
    _, fronts, width, _ = parts.shape
    out = shape_of(lax.axis_size("row"), fronts, width, NEAR * inverse.shape[2])
    return call(back_kernel, out, [], [parts, scaled, mask, inverse])


def pick_kernel(far, blocks, whole, coupling, out):
    held = whole.shape[3] // BLOCK
    for c in range(blocks.shape[0]):
        total = None
        for x in range(NEAR):
            block = blocks[c, far[0] * NEAR + x]
            lane = pl.multiple_of((block % held) * BLOCK, BLOCK)
            tile = whole[block // held, c // 2, :, pl.ds(lane, BLOCK)]
            part = dot(tile, coupling[x, c], ((1,), (0,)))
            total = part if total is None else total + part
        write_copies(out, c, total)


def pick_and_carry(far, blocks, whole, coupling):
    _, children, _, count = coupling.shape
    out = shape_of(far_size(), children, whole.shape[2], count)
    return call(pick_kernel, out, [far, blocks], [whole, coupling])


def halves(value):
    high = value.astype(BF16)
    return high, (value - high.astype(F32)).astype(BF16)


def local(
    inverse_top,
    inverse_mid,
    inverse_low,
    coupling_mid,
    coupling_low,
    source_top,
    source_mid,
    source_low,
    pivots_top,
    pivots_mid,
    pivots_low,
    sizes_mid,
    sizes_low,
    blocks_mid,
    blocks_low,
):
    row_at = lax.axis_index("row")
    col_at = lax.axis_index("col")
    far_at = col_at // NEAR
    rhs = source_top.shape[1]
    width = rhs // NEAR
    n0, n1, n2 = source_top.shape[0], source_mid.shape[1], source_low.shape[1]
    k1, k2 = inverse_mid.shape[1], inverse_low.shape[1]
    top = jnp.full((1,), inverse_top.shape[0] * lax.axis_size("row"), jnp.int32)

    far, near = far_at.reshape(1), (col_at % NEAR).reshape(1)
    table_low = update_table(blocks_low, far_at, n1 // BLOCK)
    table_mid = update_table(blocks_mid, far_at, n0 // BLOCK)
    row_mask_mid = level_mask(sizes_mid, k1, row_at * k1)
    row_mask_low = level_mask(sizes_low, k2, row_at * k2)
    col_mask_low = level_mask(sizes_low, n2, col_at * n2)
    wide_mask_mid = level_mask(sizes_mid, NEAR * n1, far_at * NEAR * n1)
    wide_mask_top = level_mask(top, NEAR * n0, far_at * NEAR * n0)

    source = jnp.swapaxes(source_low, 1, 2) * col_mask_low
    partial = jnp.einsum(
        "fij,fcj->fci", inverse_low, source.astype(BF16), preferred_element_type=F32
    )
    message = partial.astype(BF16).reshape(lax.axis_size("col"), -1, k2)

    coupling_mid_near = gather_near(coupling_mid)
    inverse_mid, source_mid, source_top, message = lax.optimization_barrier(
        (inverse_mid, source_mid, source_top, message)
    )
    others = jnp.concatenate([source_mid[0].T, source_mid[1].T, source_top.T], axis=-1)
    halved = jnp.concatenate(halves(others), axis=-1).reshape(-1, n1)
    packed = jnp.concatenate([inverse_mid.reshape(-1, n1), halved], axis=0)
    packed, inverse_top, coupling_low_late = lax.optimization_barrier(
        (packed, inverse_top, coupling_low)
    )
    packed_near = gather_near(packed)
    inverse_top_near = gather_near(inverse_top)
    coupling_low_near = gather_near(coupling_low_late)

    parts = send_col(relay_pieces(send_col(message)))
    message, scaled_low = first_update(near, parts, row_mask_low, pivots_low, coupling_low)
    message = relay_scattered(send_row(message))
    staged_mid = settled(packed_near, message)
    whole = send_col(message)

    halved = packed_near[:, 2 * k1 :].reshape(NEAR, rhs, -1)
    halved = lax.dynamic_slice_in_dim(halved, (col_at % NEAR) * width, width, 1).astype(F32)
    size = halved.shape[2] // 2
    others = halved[:, :, :size] + halved[:, :, size:]
    message = place_and_solve(table_low, whole, others, wide_mask_mid, staged_mid, 2, k1, 0)
    coupling_mid_near = settled(coupling_mid_near, message)
    parts = send_far(message)

    message, scaled_mid = update_of(parts, row_mask_mid, pivots_mid, coupling_mid_near)
    whole = send_far(relay(send_row(message)))
    inverse_top_near = settled(inverse_top_near, whole)
    k0 = inverse_top.shape[0]
    parts = send_far(
        place_and_solve(table_mid, whole, others, wide_mask_top, inverse_top_near, 1, k0, 2 * n1)
    )

    message, solution_top = relay_solved(
        send_row(root_back(parts, pivots_top, inverse_top_near)), wide_mask_top
    )
    message = pick_and_carry(far, blocks_mid, send_far(message), coupling_mid_near)
    parts = send_far(message)
    message, solution_mid = relay_solved(
        send_row(back(parts, scaled_mid, row_mask_mid, staged_mid)), wide_mask_mid
    )
    coupling_low_near = settled(coupling_low_near, message)
    parts = send_far(pick_and_carry(far, blocks_low, send_far(message), coupling_low_near))
    residual = (scaled_low - jnp.sum(parts.astype(F32), axis=0)) * row_mask_low

    upper = jnp.concatenate(
        [
            solution_top[0].reshape(width, NEAR, n0),
            solution_mid[0].reshape(width, NEAR, n1),
            solution_mid[1].reshape(width, NEAR, n1),
        ],
        axis=-1,
    )
    upper = jnp.swapaxes(jnp.concatenate(halves(upper), axis=-1), 0, 1)
    flat = jnp.swapaxes(residual, 0, 1).reshape(width, -1).astype(BF16)
    size = flat.shape[1]
    message = jnp.concatenate([copies_of(flat, NEAR), upper], axis=-1)
    got = swap_near(message)
    parts = send_row(last_product(got, inverse_low))
    upper = got[:, :, size:].astype(F32).reshape(rhs, -1)
    upper = upper[:, : upper.shape[1] // 2] + upper[:, upper.shape[1] // 2 :]
    solution_low = jnp.sum(parts.astype(F32), axis=0) * col_mask_low
    return (
        upper[:, :n0].T,
        jnp.stack([upper[:, n0 : n0 + n1].T, upper[:, n0 + n1 :].T]),
        jnp.swapaxes(solution_low, 1, 2),
    )


def solution(mesh):
    placed = (
        P("row", "col"),
        P(None, "row", "col"),
        P(None, "row", "col"),
        P(None, "col", "row"),
        P(None, "col", "row"),
        P("col", None),
        P(None, "col", None),
        P(None, "col", None),
        P("row"),
        P(None, "row"),
        P(None, "row"),
        P(),
        P(),
        P(),
        P(),
    )
    return jax.shard_map(
        local,
        mesh=mesh,
        in_specs=placed,
        out_specs=(P("col", None), P(None, "col", None), P(None, "col", None)),
        check_vma=False,
    )
```

```python
import functools

import jax
import jax.numpy as jnp
from jax import lax
from jax.experimental import pallas as pl
from jax.experimental.pallas import tpu as pltpu
from jax.sharding import PartitionSpec as P

BLOCK = 128
NEAR = 4
BF16 = jnp.bfloat16
F32 = jnp.float32
VMEM_SPEC = pl.BlockSpec(memory_space=pltpu.VMEM)
SMEM_SPEC = pl.BlockSpec(memory_space=pltpu.SMEM)


def near_groups():
    size = lax.axis_size("col")
    return [[z * NEAR + x for x in range(NEAR)] for z in range(size // NEAR)]


def far_groups():
    size = lax.axis_size("col")
    return [[z * NEAR + x for z in range(size // NEAR)] for x in range(NEAR)]


def swap_near(pieces):
    return lax.all_to_all(pieces, "col", 0, 0, axis_index_groups=near_groups(), tiled=True)


def far_size():
    return lax.axis_size("col") // NEAR


def gather_near(value):
    return lax.all_gather(value, "col", axis_index_groups=near_groups(), axis=0)


def settled(array, message):
    zero = lax.slice(message, (0,) * message.ndim, (1,) * message.ndim).reshape(()) * 0
    return array + zero.astype(array.dtype)


def settled_by(array, zeros):
    return array + zeros.reshape((1,) * (array.ndim - 1) + (-1,)).astype(array.dtype)


def copies_of(value, size):
    return jnp.broadcast_to(value.astype(BF16)[None], (size,) + value.shape)


def send_far(copies):
    groups = far_groups()
    return lax.all_to_all(copies, "col", 0, 0, axis_index_groups=groups, tiled=True)


def send_row(copies):
    return lax.all_to_all(copies, "row", 0, 0, tiled=True)


def update_table(blocks, far_at, held):
    targets = far_at * NEAR * held + jnp.arange(NEAR * held, dtype=jnp.int32)
    hits = (blocks[:, None, :] == targets[None, :, None]).astype(jnp.int32)
    return jnp.sum(hits * jnp.arange(1, blocks.shape[1] + 1, dtype=jnp.int32), axis=-1) - 1


def send_col(copies):
    return lax.all_to_all(copies, "col", 0, 0, tiled=True)


def level_mask(sizes, count, start):
    index = start + jnp.arange(count, dtype=jnp.int32)
    return (index[None, :] < sizes[:, None]).astype(F32)[:, None, :]


def dot(a, b, dims):
    return lax.dot_general(a, b, (dims, ((), ())), preferred_element_type=F32)


def call(kernel, out_shape, scalars, arrays, **static):
    return pl.pallas_call(
        functools.partial(kernel, **static),
        out_shape=out_shape,
        in_specs=[SMEM_SPEC] * len(scalars) + [VMEM_SPEC] * len(arrays),
        out_specs=jax.tree.map(lambda _: VMEM_SPEC, out_shape),
        compiler_params=pltpu.CompilerParams(vmem_limit_bytes=16 << 20),
    )(*scalars, *arrays)


LANES = 128


def tall(operand):
    missing = jnp.zeros((LANES - operand.shape[0], operand.shape[1]), F32)
    return jnp.concatenate([operand, missing], axis=0).astype(BF16)


def times_tall(matrix, operand):
    return dot(matrix, operand, ((1,), (1,)))


def arrived(parts, f):
    terms = [parts[i, f].astype(F32) for i in range(parts.shape[0])]
    while len(terms) > 1:
        terms = [terms[i] + terms[i + 1] for i in range(0, len(terms), 2)]
    return terms[0]


def write_copies(out, f, value):
    value = value.astype(BF16)
    for i in range(out.shape[0]):
        out[i, f] = value


def shape_of(*dims, dtype=BF16):
    return jax.ShapeDtypeStruct(dims, dtype)


def total_kernel(parts, out):
    terms = [parts[i].astype(F32) for i in range(parts.shape[0])]
    while len(terms) > 1:
        terms = [terms[i] + terms[i + 1] for i in range(0, len(terms), 2)]
    value = terms[0].astype(BF16)
    for i in range(out.shape[0]):
        out[i] = value


def relay_pieces(parts):
    return call(total_kernel, shape_of(*parts.shape), [], [parts])


def first_update_kernel(near, parts, mask, pivots, coupling, out, scaled):
    fronts = coupling.shape[0]
    pieces = parts.shape[0] // fronts
    share = pieces // NEAR
    for f in range(fronts):
        solved = [parts[f * pieces + g].astype(F32) for g in range(pieces)]
        operand = tall(jnp.concatenate(solved, axis=0) * mask[f])
        write_copies(out, f, times_tall(coupling[f], operand).T[: out.shape[2]])
        first = f * pieces + near[0] * share
        solved = [parts[first + g].astype(F32) for g in range(share)]
        scaled[f] = jnp.concatenate(solved, axis=0) * mask[f] * pivots[f]


def first_update(near, parts, mask, pivots, coupling):
    fronts, count, solved = coupling.shape
    rhs = parts.shape[0] * parts.shape[1] // fronts
    out = (
        shape_of(lax.axis_size("row"), fronts, rhs, count),
        shape_of(fronts, rhs // NEAR, solved, dtype=F32),
    )
    return call(first_update_kernel, out, [near], [parts, mask, pivots[:, None, :], coupling])


def last_kernel(got, inverse, out):
    count = inverse.shape[1]
    for f in range(inverse.shape[0]):
        pieces = [got[x, :, f * count : (f + 1) * count].astype(F32) for x in range(NEAR)]
        operand = jnp.concatenate(pieces, axis=0).astype(BF16)
        write_copies(out, f, dot(operand, inverse[f], ((1,), (0,))))


def last_product(got, inverse):
    fronts, _, n = inverse.shape
    out = shape_of(lax.axis_size("row"), fronts, NEAR * got.shape[1], n)
    return call(last_kernel, out, [], [got, inverse])


def scatter_kernel(parts, out, zeros):
    zeros[...] = jnp.zeros_like(zeros)
    width = out.shape[2]
    for f in range(parts.shape[1]):
        value = arrived(parts, f)
        for x in range(NEAR):
            share = value[x * width : (x + 1) * width].astype(BF16)
            for z in range(out.shape[0] // NEAR):
                out[z * NEAR + x, f] = share


def relay_scattered(parts, zeros):
    _, fronts, rhs, count = parts.shape
    out = shape_of(lax.axis_size("col"), fronts, rhs // NEAR, count)
    return call(scatter_kernel, (out, shape_of(1, zeros, dtype=F32)), [], [parts])


def update_kernel(parts, mask, pivots, coupling, out, scaled):
    for f in range(parts.shape[1]):
        solved = arrived(parts, f) * mask[f]
        scaled[f] = solved * pivots[f]
        operand = tall(solved)
        update = [times_tall(coupling[x, f], operand).T[: out.shape[2]] for x in range(NEAR)]
        write_copies(out, f, jnp.concatenate(update, axis=-1))


def update_of(parts, mask, pivots, coupling):
    _, fronts, width, count = parts.shape
    rows = lax.axis_size("row")
    out = (
        shape_of(rows, fronts, width, NEAR * coupling.shape[2]),
        shape_of(fronts, width, count, dtype=F32),
    )
    return call(update_kernel, out, [], [parts, mask, pivots[:, None, :], coupling])


def relay_kernel(parts, out):
    for f in range(parts.shape[1]):
        write_copies(out, f, arrived(parts, f))


def relay(parts):
    return call(relay_kernel, shape_of(far_size(), *parts.shape[1:]), [], [parts])


def solved_kernel(parts, mask, out, solved, zeros):
    zeros[...] = jnp.zeros_like(zeros)
    for f in range(parts.shape[1]):
        value = arrived(parts, f) * mask[f]
        solved[f] = value
        write_copies(out, f, value)


def relay_solved(parts, mask, zeros):
    shape = parts.shape[1:]
    out = (shape_of(far_size(), *shape), shape_of(*shape, dtype=F32), shape_of(1, zeros, dtype=F32))
    return call(solved_kernel, out, [], [parts, mask])


def place_kernel(table, whole, source, mask, inverse, out, zeros, *, base):
    zeros[...] = jnp.zeros_like(zeros)
    n = inverse.shape[2]
    held = n // BLOCK
    count = out.shape[3]
    spread = whole.shape[3] // BLOCK
    for p in range(out.shape[1]):
        total = None
        for x in range(NEAR):
            tiles = []
            for b in range(held):
                start = base + p * n + b * BLOCK
                tile = source[x, :, start : start + BLOCK]
                for c in (2 * p, 2 * p + 1):
                    at = table[c, x * held + b]
                    found = jnp.where(at >= 0, 1.0, 0.0).astype(F32)
                    at = jnp.maximum(at, 0)
                    if spread == 1:
                        placed = whole[at, c]
                    else:
                        lane = pl.multiple_of((at % spread) * BLOCK, BLOCK)
                        placed = whole[at // spread, c, :, pl.ds(lane, BLOCK)]
                    tile = tile - placed.astype(F32) * found
                tiles.append(tile)
            operand = jnp.concatenate(tiles, axis=-1) * mask[p, :, x * n : (x + 1) * n]
            rows = inverse[x, p * count : (p + 1) * count]
            part = times_tall(rows, tall(operand))
            total = part if total is None else total + part
        write_copies(out, p, total.T[: out.shape[2]])


def place_and_solve(table, whole, source, mask, inverse, parents, count, base, zeros):
    out = (shape_of(far_size(), parents, whole.shape[2], count), shape_of(1, zeros, dtype=F32))
    return call(place_kernel, out, [table], [whole, source, mask, inverse], base=base)


def root_kernel(parts, pivots, inverse, out):
    operand = (arrived(parts, 0) * pivots[...]).astype(BF16)
    pieces = [dot(operand, inverse[x], ((1,), (0,))) for x in range(NEAR)]
    write_copies(out, 0, jnp.concatenate(pieces, axis=-1))


def root_back(parts, pivots, inverse):
    out = shape_of(lax.axis_size("row"), 1, parts.shape[2], NEAR * inverse.shape[2])
    return call(root_kernel, out, [], [parts, pivots[None, :], inverse])


def back_kernel(parts, scaled, mask, inverse, out):
    count = parts.shape[3]
    for p in range(parts.shape[1]):
        operand = ((scaled[p] - arrived(parts, p)) * mask[p]).astype(BF16)
        pieces = [
            dot(operand, inverse[x, p * count : (p + 1) * count], ((1,), (0,)))
            for x in range(NEAR)
        ]
        write_copies(out, p, jnp.concatenate(pieces, axis=-1))


def back(parts, scaled, mask, inverse):
    _, fronts, width, _ = parts.shape
    out = shape_of(lax.axis_size("row"), fronts, width, NEAR * inverse.shape[2])
    return call(back_kernel, out, [], [parts, scaled, mask, inverse])


def pick_kernel(far, blocks, whole, coupling, out):
    held = whole.shape[3] // BLOCK
    for c in range(blocks.shape[0]):
        total = None
        for x in range(NEAR):
            block = blocks[c, far[0] * NEAR + x]
            lane = pl.multiple_of((block % held) * BLOCK, BLOCK)
            tile = whole[block // held, c // 2, :, pl.ds(lane, BLOCK)]
            part = dot(tile, coupling[x, c], ((1,), (0,)))
            total = part if total is None else total + part
        write_copies(out, c, total)


def pick_and_carry(far, blocks, whole, coupling):
    _, children, _, count = coupling.shape
    out = shape_of(far_size(), children, whole.shape[2], count)
    return call(pick_kernel, out, [far, blocks], [whole, coupling])


def halves(value):
    high = value.astype(BF16)
    return high, (value - high.astype(F32)).astype(BF16)


def local(
    inverse_top,
    inverse_mid,
    inverse_low,
    coupling_mid,
    coupling_low,
    source_top,
    source_mid,
    source_low,
    pivots_top,
    pivots_mid,
    pivots_low,
    sizes_mid,
    sizes_low,
    blocks_mid,
    blocks_low,
):
    row_at = lax.axis_index("row")
    col_at = lax.axis_index("col")
    far_at = col_at // NEAR
    rhs = source_top.shape[1]
    width = rhs // NEAR
    n0, n1, n2 = source_top.shape[0], source_mid.shape[1], source_low.shape[1]
    k1, k2 = inverse_mid.shape[1], inverse_low.shape[1]
    top = jnp.full((1,), inverse_top.shape[0] * lax.axis_size("row"), jnp.int32)

    far, near = far_at.reshape(1), (col_at % NEAR).reshape(1)
    table_low = update_table(blocks_low, far_at, n1 // BLOCK)
    table_mid = update_table(blocks_mid, far_at, n0 // BLOCK)
    row_mask_mid = level_mask(sizes_mid, k1, row_at * k1)
    row_mask_low = level_mask(sizes_low, k2, row_at * k2)
    col_mask_low = level_mask(sizes_low, n2, col_at * n2)
    wide_mask_mid = level_mask(sizes_mid, NEAR * n1, far_at * NEAR * n1)
    wide_mask_top = level_mask(top, NEAR * n0, far_at * NEAR * n0)

    source = jnp.swapaxes(source_low, 1, 2) * col_mask_low
    partial = jnp.einsum(
        "fij,fcj->fci", inverse_low, source.astype(BF16), preferred_element_type=F32
    )
    message = partial.astype(BF16).reshape(lax.axis_size("col"), -1, k2)

    coupling_mid_near = gather_near(coupling_mid)
    inverse_mid, source_mid, source_top, message = lax.optimization_barrier(
        (inverse_mid, source_mid, source_top, message)
    )
    others = jnp.concatenate([source_mid[0].T, source_mid[1].T, source_top.T], axis=-1)
    halved = jnp.concatenate(halves(others), axis=-1).reshape(-1, n1)
    packed = jnp.concatenate([inverse_mid.reshape(-1, n1), halved], axis=0)
    packed, inverse_top, coupling_low_late = lax.optimization_barrier(
        (packed, inverse_top, coupling_low)
    )
    packed_near = gather_near(packed)
    inverse_top_near = gather_near(inverse_top)
    coupling_low_near = gather_near(coupling_low_late)

    parts = send_col(relay_pieces(send_col(message)))
    message, scaled_low = first_update(near, parts, row_mask_low, pivots_low, coupling_low)
    message, zeros = relay_scattered(send_row(message), n1)
    staged_mid = settled_by(packed_near, zeros)
    whole = send_col(message)

    halved = packed_near[:, 2 * k1 :].reshape(NEAR, rhs, -1)
    halved = lax.dynamic_slice_in_dim(halved, (col_at % NEAR) * width, width, 1).astype(F32)
    size = halved.shape[2] // 2
    others = halved[:, :, :size] + halved[:, :, size:]
    message, zeros = place_and_solve(
        table_low, whole, others, wide_mask_mid, staged_mid, 2, k1, 0, k1
    )
    coupling_mid_near = settled_by(coupling_mid_near, zeros)
    parts = send_far(message)

    message, scaled_mid = update_of(parts, row_mask_mid, pivots_mid, coupling_mid_near)
    whole = send_far(relay(send_row(message)))
    inverse_top_near = settled(inverse_top_near, whole)
    k0 = inverse_top.shape[0]
    message, _ = place_and_solve(
        table_mid, whole, others, wide_mask_top, inverse_top_near, 1, k0, 2 * n1, k1
    )
    parts = send_far(message)

    message, solution_top, _ = relay_solved(
        send_row(root_back(parts, pivots_top, inverse_top_near)), wide_mask_top, k2
    )
    message = pick_and_carry(far, blocks_mid, send_far(message), coupling_mid_near)
    parts = send_far(message)
    message, solution_mid, zeros = relay_solved(
        send_row(back(parts, scaled_mid, row_mask_mid, staged_mid)), wide_mask_mid, k2
    )
    coupling_low_near = settled_by(coupling_low_near, zeros)
    parts = send_far(pick_and_carry(far, blocks_low, send_far(message), coupling_low_near))
    residual = (scaled_low - jnp.sum(parts.astype(F32), axis=0)) * row_mask_low

    upper = jnp.concatenate(
        [
            solution_top[0].reshape(width, NEAR, n0),
            solution_mid[0].reshape(width, NEAR, n1),
            solution_mid[1].reshape(width, NEAR, n1),
        ],
        axis=-1,
    )
    upper = jnp.swapaxes(jnp.concatenate(halves(upper), axis=-1), 0, 1)
    flat = jnp.swapaxes(residual, 0, 1).reshape(width, -1).astype(BF16)
    size = flat.shape[1]
    message = jnp.concatenate([copies_of(flat, NEAR), upper], axis=-1)
    got = swap_near(message)
    parts = send_row(last_product(got, inverse_low))
    upper = got[:, :, size:].astype(F32).reshape(rhs, -1)
    upper = upper[:, : upper.shape[1] // 2] + upper[:, upper.shape[1] // 2 :]
    solution_low = jnp.sum(parts.astype(F32), axis=0) * col_mask_low
    return (
        upper[:, :n0].T,
        jnp.stack([upper[:, n0 : n0 + n1].T, upper[:, n0 + n1 :].T]),
        jnp.swapaxes(solution_low, 1, 2),
    )


def solution(mesh):
    placed = (
        P("row", "col"),
        P(None, "row", "col"),
        P(None, "row", "col"),
        P(None, "col", "row"),
        P(None, "col", "row"),
        P("col", None),
        P(None, "col", None),
        P(None, "col", None),
        P("row"),
        P(None, "row"),
        P(None, "row"),
        P(),
        P(),
        P(),
        P(),
    )
    return jax.shard_map(
        local,
        mesh=mesh,
        in_specs=placed,
        out_specs=(P("col", None), P(None, "col", None), P(None, "col", None)),
        check_vma=False,
    )
```
